256 devices in a mesh: row: 8 (over y, core), band: 32 (over z, x).
Axes of the slice: x: 4, y: 4, z: 8, core: 2. Of those that a mesh axis runs over, the one named last changes fastest.
Arguments:
- coeffs: bfloat16 [8192, 16384], P('row', 'band'), may hold values from -0.046875 to 0.046875
- occupation: float32 [16384], P('band'), may hold values from 0.2 to 2
- tile_left: int32 [8, 8, 16], P('row'), may hold values from 0 to 7
- tile_right: int32 [8, 8, 16], P('row'), may hold values from 0 to 7
- owners: int32 [1024, 6], P(('row', 'band')), may hold values from 0 to 31, all different within a row; in each aligned block of 4 rows (0 to 3, 4 to 7, ...) at most 2 rows name the same one
- brick_slot: int32 [1024, 6], P(('row', 'band')), may hold values from 0 to 7
- patterns: int32 [1024, 6, 2], P(('row', 'band')), may hold values from 0 to 3
- basis_table: bfloat16 [4, 128, 2048], replicated, may hold values from -3 to 3
Outputs:
- density: float32 [2048, 2048], P(('row', 'band'))
The draws below stay inside these ranges and needn't reach their ends.
Inputs may be any that keep to these rules, and one draw needn't show every extreme that they name: Each row names 6 different owners. Among the rows g from k * 4 to k * 4 + 4 - 1 (aligned blocks), no owner is named by more than 2 rows, a bound that some owner reaches in some of these blocks.
All inputs are finite; a program needn't handle non-finite values.
Results may differ from the reference program's by a relative error of at most 0.009.
Values may be sent and summed in bfloat16 or wider, within the bound.
A program may use at most 64 MiB of HBM per device.

```python
import math
import jax
import jax.numpy as jnp
import numpy as np
from jax import lax

BS = 128
NB_DEV = 8
BAND_DEV = 512
NT_DEV = 4
TOP = 6
NBR_DEV = 8
G = 2048
PATTERNS = 4
NBAS = 8192
NOCC = 16384
NTP = 16
TILES = 1024
CAP = 2
BRICKS = 2048
N_ROW = 8
N_BAND = 32


def set_ends(values, own_key, least, high):
    extent = values.shape
    index_at = [jax.random.randint(jax.random.fold_in(own_key, axis), (), 0, extent[axis]) for axis in range(len(extent))]
    values = values.at[tuple(index_at)].set(least)
    longest = extent.index(max(extent))
    index_at[longest] = (index_at[longest] + 1) % extent[longest]
    return values.at[tuple(index_at)].set(high)


def shard_levels(own_key, dims, pieces, low, top_value):
    def one(position, shards_of):
        heights = jax.random.uniform(jax.random.fold_in(jax.random.fold_in(own_key, 6), position), (shards_of,), jnp.float32, low / len(pieces), top_value / len(pieces))
        return jnp.repeat(jnp.exp(heights), dims[position] // shards_of).reshape((-1,) + (1,) * (len(dims) - position - 1))

    gain = one(*pieces[0])
    for cut in pieces[1:]:
        gain = gain * one(*cut)
    return gain


def deal_out(stream_key, own, number, rows, number_of, top, limit, lean):
    order = jax.random.permutation(stream_key, number_of)
    crowded, ordinary = shares(number_of, rows * top, limit, lean, True), shares(number_of, rows * top, limit, lean, False)
    places = jnp.arange(number_of)

    def named(lengths, offset_by):
        used = int((lengths > 0).sum())
        fixed = max(1, used // 4)
        moved = fixed + (places - fixed + offset_by * (used - fixed)) % max(1, number_of - fixed)
        return jnp.zeros((number_of,), jnp.int32).at[order[jnp.where(places < fixed, places, moved)]].set(jnp.asarray(lengths, jnp.int32))

    lengths = jnp.where(number % 4 == 0, named(crowded, number // 4), named(ordinary, number - number // 4 - 1))
    mixed = jax.random.permutation(jax.random.fold_in(own, 3), number_of)
    donor, sink = mixed[0:number_of // 2 * 2:2], mixed[1:number_of // 2 * 2:2]
    slack = jnp.minimum(lengths[donor] - 1, limit - lengths[sink]) // 2
    slack = jnp.where((donor == order[0]) | (sink == order[0]) | (lengths[sink] == 0), 0, jnp.maximum(slack, 0))
    moved = jax.random.randint(jax.random.fold_in(own, 4), (number_of // 2,), 0, 1 << 20) % (slack + 1)
    lengths = lengths.at[donor].add(-moved).at[sink].add(moved)
    items = jnp.searchsorted(jnp.cumsum(lengths), jnp.arange(rows * top), side="right").astype(jnp.int32)
    grid = items.reshape(top, rows).T
    grid = grid[jax.random.permutation(jax.random.fold_in(own, 1), rows)]
    offset_by = jax.random.randint(jax.random.fold_in(own, 2), (rows, 1), 0, top)
    return jnp.take_along_axis(grid, (jnp.arange(top)[None, :] + offset_by) % top, axis=1)


def shares(count, total, reach, slope, full):
    weights = [(1 << 20) // math.isqrt(standing ** slope) + 1 for standing in range(1, count + 1)]
    largest = reach if full else min(reach, max(-(-total // count), total * weights[0] // sum(weights)))
    least = 1 if total - largest >= count - 1 else 0
    holding, spare = [largest] + [least] * (count - 1), total - largest - least * (count - 1)
    while spare > 0:
        movable = [i for i in range(1, count) if holding[i] < largest] or [i for i in range(1, count) if holding[i] < reach]
        pool, left = sum([weights[i] for i in movable]), spare
        for i in movable:
            more = min(reach - holding[i], max(1, left * weights[i] // pool), spare)
            holding[i] = holding[i] + more
            spare = spare - more
    return np.array(holding)


def noise(rng, dims, spread, reach, pieces=(), kind=jnp.bfloat16):
    array = jax.random.normal(rng, dims, jnp.float32) * spread
    if len(pieces) > 0:
        array = shard_levels(rng, dims, pieces, -0.22, 0.18) * array
    return jnp.clip(array, min=-reach, max=reach).astype(kind)


def setup_inputs(seed: int = 0) -> dict:
    keys = jax.random.split(jax.random.key(seed), 9)
    coeffs = noise(keys[0], (NBAS, NOCC), NOCC ** -0.5, 0.046875, ((0, 8), (1, 32)))
    occupation = jnp.clip(0.2 + 1.8 * jax.random.uniform(keys[1], (NOCC,), jnp.float32) ** shard_levels(keys[1], (NOCC,), ((0, 32),), -0.2, 0.2), 0.2, 2.0)
    tile_left = set_ends(jax.random.randint(keys[2], (N_ROW, N_ROW, NTP), 0, NB_DEV), jax.random.fold_in(keys[2], 1), 0, NB_DEV - 1).astype(jnp.int32)
    tile_right = set_ends(jax.random.randint(keys[3], (N_ROW, N_ROW, NTP), 0, NB_DEV), jax.random.fold_in(keys[3], 1), 0, NB_DEV - 1).astype(jnp.int32)
    owners_keys = jax.random.split(jax.random.fold_in(keys[4], 1), TILES // NT_DEV)
    owners_turns = jax.random.permutation(jax.random.fold_in(keys[4], 3), TILES // NT_DEV)
    owners = jax.vmap(lambda own, number: deal_out(jax.random.fold_in(keys[4], 2), own, number, NT_DEV, N_BAND, TOP, CAP, 2))(owners_keys, owners_turns).reshape((TILES, TOP))
    brick_slot = set_ends(jax.random.randint(keys[5], (TILES, TOP), 0, NBR_DEV), jax.random.fold_in(keys[5], 1), 0, NBR_DEV - 1).astype(jnp.int32)
    patterns = set_ends(jax.random.randint(keys[6], (TILES, TOP, 2), 0, PATTERNS), jax.random.fold_in(keys[6], 1), 0, PATTERNS - 1).astype(jnp.int32)
    basis_table = noise(keys[7], (PATTERNS, BS, G), 0.5, 3.0)
    return dict(coeffs=coeffs, occupation=occupation, tile_left=tile_left, tile_right=tile_right, owners=owners, brick_slot=brick_slot, patterns=patterns, basis_table=basis_table)


def reference(coeffs, occupation, tile_left, tile_right, owners, brick_slot, patterns, basis_table):
    weighted = (coeffs.astype(jnp.float32) * occupation[None, :]).astype(jnp.bfloat16)
    lefts = tile_left.reshape(-1).astype(jnp.int32)
    rights = tile_right.reshape(-1).astype(jnp.int32)
    count = lefts.shape[0]
    order = jnp.arange(count, dtype=jnp.int32)
    row_of = order // (N_ROW * NTP)
    col_of = (order // NTP) % N_ROW
    first = ((row_of * NB_DEV + lefts) * BS).astype(jnp.int32)
    second = ((col_of * NB_DEV + rights) * BS).astype(jnp.int32)
    weight = jnp.where((row_of == col_of) & (lefts == rights), 1.0, 2.0).astype(jnp.float32)
    targets = ((row_of[:, None] * N_BAND + owners.astype(jnp.int32)) * NBR_DEV + brick_slot.astype(jnp.int32)).astype(jnp.int32)

    def step(density, item):
        start_left, start_right, scale, target, pattern = item
        rows_left = lax.dynamic_slice_in_dim(weighted, start_left, BS, 0).astype(jnp.float32).reshape(BS, N_BAND, BAND_DEV)
        rows_right = lax.dynamic_slice_in_dim(coeffs, start_right, BS, 0).astype(jnp.float32).reshape(BS, N_BAND, BAND_DEV)
        parts = jnp.einsum('ibk,jbk->bij', rows_left, rows_right)
        parts = lax.optimization_barrier(parts.astype(jnp.bfloat16)).astype(jnp.float32)
        block = jnp.sum(parts, axis=0).astype(jnp.bfloat16)
        for slot in range(TOP):
            products = jnp.dot(block, basis_table[pattern[slot, 1]], preferred_element_type=jnp.float32)
            term = jnp.sum(basis_table[pattern[slot, 0]].astype(jnp.float32) * products, axis=0) * scale
            density = density.at[target[slot]].add(term)
        return density, None

    density = jnp.zeros((BRICKS, G), jnp.float32)
    density, unused = lax.scan(step, density, (first, second, weight, targets, patterns.astype(jnp.int32)))
    return density
```

```python
import functools

import jax
import jax.numpy as jnp
from jax import lax
from jax.experimental import pallas as pl
from jax.experimental.pallas import tpu as pltpu
from jax.sharding import PartitionSpec as P

BS = 128
NBR = 8
TOP = 6
G = 2048
GS, GL = 16, 128
NTP = 16
BLOCKS = 8
KD = 512
NX, NY, NZ = 4, 4, 8
CHUNK = 512
Z_ORDER = (4, 3, 5, 2, 6, 1, 7)
X_ORDER = (2, 1, 3)
MESH = pl.DeviceIdType.MESH


def kernel(
    coeffs,
    occ,
    left,
    right,
    meta,
    basis,
    out,
    w,
    b0,
    f_a,
    f_b,
    s_a,
    s_b,
    t_a,
    t_b,
    tiles,
    x1_l,
    x1_r,
    x2_l,
    x2_r,
    zs,
    rz,
    terms,
    send_e,
    e1,
    arr,
    mx,
    mz,
    hits,
    meta_s,
    g_send,
    g_recv,
    x_send,
    x_recv,
    z_send,
    z_recv,
    e_send,
    e_recv,
    m_send,
    m_recv,
    l_sem,
):
    r = lax.axis_index("row")
    band = lax.axis_index("band")
    y, c = r // 2, r % 2
    z, x = band // NX, band % NX
    sg = 1 - 2 * c
    yp, ym, y2 = (y + sg + NY) % NY, (y - sg + NY) % NY, (y + 2) % NY
    oc = 1 - c
    xr, xl, x2 = (x + 1) % NX, (x + 3) % NX, (x + 2) % NX

    def dev_row(rr):
        return (rr, band)

    def dev_x(xx):
        return (r, z * NX + xx)

    def dev_z(zz):
        return (r, zz * NX + x)

    sib = dev_row(2 * y + oc)
    dyp = dev_row(2 * yp + c)
    dym = dev_row(2 * ym + c)

    def remote(src, dst, ss, rs, dev):
        return pltpu.make_async_remote_copy(
            src_ref=src, dst_ref=dst, send_sem=ss, recv_sem=rs, device_id=dev, device_id_type=MESH
        )

    barrier = pltpu.get_barrier_semaphore()
    peers = [sib, dyp, dym]
    peers += [dev_x((x + d) % NX) for d in X_ORDER]
    peers += [dev_z((z + d) % NZ) for d in Z_ORDER]
    for p in peers:
        pl.semaphore_signal(barrier, inc=1, device_id=p, device_id_type=MESH)

    w[...] = (coeffs[...].astype(jnp.float32) * occ[...]).astype(jnp.bfloat16)
    mx[x] = meta[...]
    pl.semaphore_wait(barrier, len(peers))

    pending = []
    g_p = remote(coeffs, f_a, g_send.at[0], g_recv.at[0], dyp)
    g_p.start()
    g_s = remote(coeffs, b0, g_send.at[1], g_recv.at[1], sib)
    g_s.start()
    m_x = [
        remote(mx.at[x], mx.at[x], m_send.at[d], m_recv.at[d], dev_x((x + d) % NX)) for d in X_ORDER
    ]
    for m in m_x:
        m.start()

    def compute_tiles(panel, k, j, s):
        def one(p, carry):
            a = w[left[s, p]]
            b = panel[right[s, p]]
            t = lax.dot_general(
                a, b, (((1,), (1,)), ((), ())), preferred_element_type=jnp.float32
            )
            tiles[k, p // 4, (p // 2) % 2, j, p % 2] = t.astype(jnp.bfloat16)
            return carry

        lax.fori_loop(0, NTP, one, 0)

    x1 = {}
    x2c = {}
    zc = {}
    e1c = {}
    e2c = {}

    def x1_start(k):
        x1[k] = (
            remote(tiles.at[k, x2, 0], x1_l.at[k], x_send.at[k, 0], x_recv.at[k, 0], dev_x(xr)),
            remote(tiles.at[k, x2, 1], x1_r.at[k], x_send.at[k, 1], x_recv.at[k, 1], dev_x(xl)),
        )
        for q in x1[k]:
            q.start()

    def x2_start(k):
        to_r = remote(tiles.at[k, xr], x2_l.at[k], x_send.at[k, 2], x_recv.at[k, 2], dev_x(xr))
        to_l = remote(tiles.at[k, xl], x2_r.at[k], x_send.at[k, 3], x_recv.at[k, 3], dev_x(xl))
        for half, dst, first, second in ((0, xr, x1[k][0], to_r), (1, xl, x1[k][1], to_l)):
            first.wait_recv()
            got = (x1_l, x1_r)[half]
            tiles[k, dst, half] = (
                tiles[k, dst, half].astype(jnp.float32) + got[k].astype(jnp.float32)
            ).astype(jnp.bfloat16)
            second.start()
        x2c[k] = (to_r, to_l)

    def z_start(k):
        for q in x2c[k]:
            q.wait_recv()
        for j in range(2):
            for h in range(2):
                total = (
                    tiles[k, x, h, j].astype(jnp.float32)
                    + x2_l[k, h, j].astype(jnp.float32)
                    + x2_r[k, h, j].astype(jnp.float32)
                )
                zs[k, pl.ds(4 * j + 2 * h, 2)] = total.astype(jnp.bfloat16)
        cs = []
        for d in Z_ORDER:
            to = (z + d) % NZ
            q = remote(zs.at[k, to], rz.at[k, z], z_send.at[k, d], z_recv.at[k, d], dev_z(to))
            q.start()
            cs.append(q)
        rz[k, z] = zs[k, z]
        zc[k] = cs

    sj = z // 4
    si = z % 4

    def panel_of(k, j):
        if k == 0:
            a, b = 2 * y + c, 2 * y + oc
        elif k == 1:
            a, b = 2 * ym + c, 2 * yp + oc
        elif k == 2:
            a, b = 2 * yp + c, 2 * ym + oc
        else:
            a, b = 2 * y2 + c, 2 * y2 + oc
        return a if j == 0 else b

    def my_panel(k):
        return panel_of(k, 0) * (1 - sj) + panel_of(k, 1) * sj

    def collocate(k):
        for q in zc[k]:
            q.wait_recv()
        block = jnp.sum(rz[k].astype(jnp.float32), axis=0).astype(jnp.bfloat16)
        s = my_panel(k)
        p = 4 * x + si
        same = jnp.logical_and(s == r, left[s, p] == right[s, p])
        scale = jnp.where(same, 1.0, 2.0).astype(jnp.float32)

        def one(t, carry):
            pa = meta_s[k, si, 12 + t]
            pb = meta_s[k, si, 18 + t]
            for ch in range(G // CHUNK):
                cols = pl.ds(ch * CHUNK, CHUNK)
                prod = jnp.dot(block, basis[pb, :, cols], preferred_element_type=jnp.float32)
                row = jnp.sum(basis[pa, :, cols].astype(jnp.float32) * prod, axis=0, keepdims=True)
                row = row * scale
                for q in range(CHUNK // GL):
                    terms[k, t, pl.ds(ch * (CHUNK // GL) + q, 1), :] = row[:, q * GL : (q + 1) * GL]
            return carry

        lax.fori_loop(0, TOP, one, 0)
        vals = [terms[k, t] for t in range(TOP)]
        own = [meta_s[k, si, t] for t in range(TOP)]

        def place(o, carry):
            acc = jnp.zeros((GS, GL), jnp.float32)
            for t in range(TOP):
                acc = jnp.where(own[t] == o, vals[t], acc)
            send_e[k, o % NX, o // NX] = acc.astype(jnp.bfloat16)
            return carry

        lax.fori_loop(0, NX * NZ, place, 0)
        cs = []
        for d in X_ORDER:
            to = (x + d) % NX
            q = remote(send_e.at[k, to], e1.at[k, x], e_send.at[k, d], e_recv.at[k, d], dev_x(to))
            q.start()
            cs.append(q)
        e1[k, x] = send_e[k, x]
        e1c[k] = cs

    def e2_start(k):
        for q in e1c[k]:
            q.wait_recv()
        cs = []
        for d in Z_ORDER:
            to = (z + d) % NZ
            q = remote(
                e1.at[k, :, to], arr.at[k, z], e_send.at[k, 4 + d], e_recv.at[k, 4 + d], dev_z(to)
            )
            q.start()
            cs.append(q)
        arr[k, z] = e1[k, :, z]
        e2c[k] = cs

    def finish(k, acc):
        for q in e2c[k]:
            q.wait_recv()

        def one(i, acc):
            zf, xf = i // NX, i % NX
            jj = zf // 4
            ii = zf % 4
            s = panel_of(k, 0) * (1 - jj) + panel_of(k, 1) * jj
            val = arr[k, zf, xf].astype(jnp.float32)
            slot = hits[s, xf, pl.ds(ii, 1), :]
            return tuple(acc[b] + jnp.where(slot == float(b), val, 0.0) for b in range(NBR))

        return lax.fori_loop(0, NX * NZ, one, acc)

    compute_tiles(coeffs, 0, 0, panel_of(0, 0))
    for m in m_x:
        m.wait_recv()
    m_z = []
    for d in Z_ORDER:
        to = (z + d) % NZ
        q = remote(mx, mz.at[z], m_send.at[4 + d], m_recv.at[4 + d], dev_z(to))
        q.start()
        m_z.append(q)
    mz[z] = mx[...]
    g_s.wait_recv()
    compute_tiles(b0, 0, 1, panel_of(0, 1))
    x1_start(0)
    for q in m_z:
        q.wait_recv()
    locals_ = []
    for k in range(4):
        q = pltpu.make_async_copy(mz.at[my_panel(k), x], meta_s.at[k], l_sem.at[k])
        q.start()
        locals_.append(q)

    lane = lax.broadcasted_iota(jnp.int32, (8, 128), 1)

    def hit(i, carry):
        zf, xf = i // NX, i % NX
        m = mz[zf, xf]
        slots = pltpu.roll(m, 128 - TOP, axis=1)
        mine = jnp.logical_and(lane < TOP, m == band)
        val = jnp.where(mine, slots + 1, 0).astype(jnp.float32)
        hits[zf, xf] = jnp.broadcast_to(jnp.sum(val, axis=1, keepdims=True) - 1.0, (8, 128))
        return carry

    lax.fori_loop(0, NX * NZ, hit, 0)
    for q in locals_:
        q.wait()
    x2_start(0)
    g_p.wait_send()
    g_m = remote(coeffs, s_a, g_send.at[2], g_recv.at[2], dym)
    g_m.start()

    g_p.wait_recv()
    g_fs = remote(f_a, f_b, g_send.at[3], g_recv.at[3], sib)
    g_fs.start()
    top = pl.ds(0, BLOCKS // 2)
    low = pl.ds(BLOCKS // 2, BLOCKS // 2)
    g_f = remote(f_a.at[top], t_a.at[top], g_send.at[4], g_recv.at[4], dyp)
    g_f.start()
    compute_tiles(f_a, 1, 0, panel_of(1, 0))
    z_start(0)
    g_fs.wait_recv()
    compute_tiles(f_b, 1, 1, panel_of(1, 1))
    x1_start(1)

    g_m.wait_recv()
    g_ms = remote(s_a, s_b, g_send.at[5], g_recv.at[5], sib)
    g_ms.start()
    g_b = remote(s_a.at[low], t_a.at[low], g_send.at[6], g_recv.at[6], dym)
    g_b.start()
    x2_start(1)
    compute_tiles(s_a, 2, 0, panel_of(2, 0))
    g_ms.wait_recv()
    compute_tiles(s_b, 2, 1, panel_of(2, 1))
    x1_start(2)
    z_start(1)
    collocate(0)

    g_f.wait_recv()
    g_b.wait_recv()
    g_ts = remote(t_a, t_b, g_send.at[7], g_recv.at[7], sib)
    g_ts.start()
    x2_start(2)
    compute_tiles(t_a, 3, 0, panel_of(3, 0))
    g_ts.wait_recv()
    compute_tiles(t_b, 3, 1, panel_of(3, 1))
    x1_start(3)
    z_start(2)
    e2_start(0)
    collocate(1)
    x2_start(3)
    e2_start(1)
    collocate(2)
    z_start(3)
    e2_start(2)
    acc = tuple(jnp.zeros((GS, GL), jnp.float32) for _ in range(NBR))
    acc = finish(0, acc)
    collocate(3)
    e2_start(3)
    acc = finish(1, acc)
    acc = finish(2, acc)
    acc = finish(3, acc)
    for b in range(NBR):
        out[b] = acc[b]

    pending += [g_p, g_s, g_m, g_fs, g_f, g_ms, g_b, g_ts] + m_x + m_z
    for k in range(4):
        pending += list(x1[k]) + list(x2c[k]) + zc[k] + e1c[k] + e2c[k]
    for q in pending:
        if q is not g_p:
            q.wait_send()


def body(coeffs, occupation, tile_left, tile_right, owners, brick_slot, patterns, basis_table):
    meta = jnp.concatenate([owners, brick_slot, patterns[:, :, 0], patterns[:, :, 1]], axis=1)
    meta = jnp.pad(meta, ((0, 4), (0, 128 - 4 * TOP)))
    vm = pl.BlockSpec(memory_space=pltpu.VMEM)
    sm = pl.BlockSpec(memory_space=pltpu.SMEM)
    bf, f32 = jnp.bfloat16, jnp.float32
    panel = pltpu.VMEM((BLOCKS, BS, KD), bf)
    out = pl.pallas_call(
        kernel,
        out_shape=jax.ShapeDtypeStruct((NBR, GS, GL), f32),
        in_specs=[vm, vm, sm, sm, vm, vm],
        out_specs=vm,
        scratch_shapes=[panel] * 8
        + [
            pltpu.VMEM((4, NX, 2, 2, 2, BS, BS), bf),
            pltpu.VMEM((4, 2, 2, BS, BS), bf),
            pltpu.VMEM((4, 2, 2, BS, BS), bf),
            pltpu.VMEM((4, 2, 2, 2, BS, BS), bf),
            pltpu.VMEM((4, 2, 2, 2, BS, BS), bf),
            pltpu.VMEM((4, NZ, BS, BS), bf),
            pltpu.VMEM((4, NZ, BS, BS), bf),
            pltpu.VMEM((4, TOP, GS, GL), f32),
            pltpu.VMEM((4, NX, NZ, GS, GL), bf),
            pltpu.VMEM((4, NX, NZ, GS, GL), bf),
            pltpu.VMEM((4, NZ, NX, GS, GL), bf),
            pltpu.VMEM((NX, 8, 128), jnp.int32),
            pltpu.VMEM((NZ, NX, 8, 128), jnp.int32),
            pltpu.VMEM((NZ, NX, 8, 128), f32),
            pltpu.SMEM((4, 8, 128), jnp.int32),
            pltpu.SemaphoreType.DMA((8,)),
            pltpu.SemaphoreType.DMA((8,)),
            pltpu.SemaphoreType.DMA((4, 4)),
            pltpu.SemaphoreType.DMA((4, 4)),
            pltpu.SemaphoreType.DMA((4, NZ)),
            pltpu.SemaphoreType.DMA((4, NZ)),
            pltpu.SemaphoreType.DMA((4, 12)),
            pltpu.SemaphoreType.DMA((4, 12)),
            pltpu.SemaphoreType.DMA((12,)),
            pltpu.SemaphoreType.DMA((12,)),
            pltpu.SemaphoreType.DMA((4,)),
        ],
        compiler_params=pltpu.CompilerParams(
            collective_id=0, has_side_effects=True, vmem_limit_bytes=50 * 1024 * 1024
        ),
        cost_estimate=pl.CostEstimate(
            flops=4 * 10**9, bytes_accessed=4 * 10**6, transcendentals=0
        ),
    )(
        coeffs.reshape(BLOCKS, BS, KD),
        occupation.reshape(1, KD),
        tile_left[0],
        tile_right[0],
        meta,
        basis_table,
    )
    return out.reshape(NBR, G)


def solution(mesh):
    return jax.shard_map(
        body,
        mesh=mesh,
        in_specs=(
            P("row", "band"),
            P("band"),
            P("row", None, None),
            P("row", None, None),
            P(("row", "band"), None),
            P(("row", "band"), None),
            P(("row", "band"), None, None),
            P(),
        ),
        out_specs=P(("row", "band"), None),
        check_vma=False,
    )
```

```python
import jax
import jax.numpy as jnp
from jax import lax
from jax.experimental import pallas as pl
from jax.experimental.pallas import tpu as pltpu
from jax.sharding import PartitionSpec as P

BS = 128
NBR = 8
TOP = 6
G = 2048
GS, GL = 16, 128
NTP = 16
BLOCKS = 8
KD = 512
NX, NY, NZ = 4, 4, 8
CHUNK = 512
Z_ORDER = (4, 3, 5, 2, 6, 1, 7)
X_ORDER = (2, 1, 3)
E_ORDER = tuple(zz * NX + xx for zz in Z_ORDER + (0,) for xx in (2, 1, 3, 0) if zz or xx)
VMEM = 62 * 2**20
MESH = pl.DeviceIdType.MESH


def kernel(
    coeffs_hbm,
    occ_hbm,
    left_hbm,
    right_hbm,
    meta_hbm,
    basis_hbm,
    out,
    coeffs,
    occ,
    basis,
    w,
    b0,
    f_a,
    f_b,
    s_a,
    s_b,
    t_a,
    t_b,
    tiles,
    x1_l,
    x1_r,
    x2_l,
    x2_r,
    zs,
    rz,
    terms,
    send_e,
    arr,
    mx,
    mz,
    hits,
    meta_s,
    left_s,
    right_s,
    g_send,
    g_recv,
    x_send,
    x_recv,
    z_send,
    z_recv,
    e_send,
    e_recv,
    m_send,
    m_recv,
    l_sem,
    i_sem,
):
    r = lax.axis_index("row")
    band = lax.axis_index("band")
    y, c = r // 2, r % 2
    z, x = band // NX, band % NX
    sg = 1 - 2 * c
    yp, ym, y2 = (y + sg + NY) % NY, (y - sg + NY) % NY, (y + 2) % NY
    oc = 1 - c
    xr, xl, x2 = (x + 1) % NX, (x + 3) % NX, (x + 2) % NX

    def dev_row(rr):
        return (rr, band)

    def dev_x(xx):
        return (r, z * NX + xx)

    def dev_at(zz, xx):
        return (r, zz * NX + xx)

    def dev_z(zz):
        return (r, zz * NX + x)

    sib = dev_row(2 * y + oc)
    dyp = dev_row(2 * yp + c)
    dym = dev_row(2 * ym + c)

    def remote(src, dst, ss, rs, dev):
        return pltpu.make_async_remote_copy(
            src_ref=src, dst_ref=dst, send_sem=ss, recv_sem=rs, device_id=dev, device_id_type=MESH
        )

    barrier = pltpu.get_barrier_semaphore()
    peers = [sib, dyp, dym]
    peers += [dev_at((z + d // NX) % NZ, (x + d) % NX) for d in range(1, NX * NZ)]
    for p in peers:
        pl.semaphore_signal(barrier, inc=1, device_id=p, device_id_type=MESH)

    loads = [
        pltpu.make_async_copy(src, dst, i_sem.at[i])
        for i, (src, dst) in enumerate(
            (
                (coeffs_hbm, coeffs),
                (occ_hbm, occ),
                (left_hbm, left_s),
                (right_hbm, right_s),
                (meta_hbm, mx.at[x]),
                (basis_hbm, basis),
            )
        )
    ]
    for q in loads:
        q.start()
    for q in loads[:5]:
        q.wait()
    w[...] = (coeffs[...].astype(jnp.float32) * occ[...]).astype(jnp.bfloat16)
    pl.semaphore_wait(barrier, len(peers))

    pending = []
    halves = (pl.ds(0, BLOCKS // 2), pl.ds(BLOCKS // 2, BLOCKS // 2))
    g_s = remote(coeffs_hbm, b0, g_send.at[0], g_recv.at[0], sib)
    g_p = [
        remote(coeffs_hbm.at[v], f_a.at[v], g_send.at[1 + i], g_recv.at[1 + i], dyp)
        for i, v in enumerate(halves)
    ]
    g_m = [
        remote(coeffs_hbm.at[v], s_a.at[v], g_send.at[3 + i], g_recv.at[3 + i], dym)
        for i, v in enumerate(halves)
    ]
    m_x = [
        remote(mx.at[x], mx.at[x], m_send.at[d], m_recv.at[d], dev_x((x + d) % NX)) for d in X_ORDER
    ]
    g_s.start()
    for q in g_p + m_x:
        q.start()

    def compute_tiles(panel, h, s):
        def one(p, carry):
            a = w[left_s[0, s, p]]
            b = panel[right_s[0, s, p]]
            t = lax.dot_general(
                a, b, (((1,), (1,)), ((), ())), preferred_element_type=jnp.float32
            )
            tiles[h, p // 4, p % 4] = t.astype(jnp.bfloat16)
            return carry

        lax.fori_loop(0, NTP, one, 0)

    x1 = {}
    x2c = {}
    top, low = pl.ds(0, 2), pl.ds(2, 2)

    def x1_start(h):
        x1[h] = (
            remote(tiles.at[h, x2, top], x1_l.at[h], x_send.at[h, 0], x_recv.at[h, 0], dev_x(xr)),
            remote(tiles.at[h, x2, low], x1_r.at[h], x_send.at[h, 1], x_recv.at[h, 1], dev_x(xl)),
        )
        for q in x1[h]:
            q.start()

    def x2_start(h):
        to_r = remote(tiles.at[h, xr], x2_l.at[h], x_send.at[h, 2], x_recv.at[h, 2], dev_x(xr))
        to_l = remote(tiles.at[h, xl], x2_r.at[h], x_send.at[h, 3], x_recv.at[h, 3], dev_x(xl))
        for part, dst, got, first, second in (
            (top, xr, x1_l, x1[h][0], to_r),
            (low, xl, x1_r, x1[h][1], to_l),
        ):
            first.wait_recv()
            tiles[h, dst, part] = (
                tiles[h, dst, part].astype(jnp.float32) + got[h].astype(jnp.float32)
            ).astype(jnp.bfloat16)
            second.start()
        x2c[h] = (to_r, to_l)

    def z_copy(h, i):
        to = 4 * (h % 2) + i
        return remote(
            zs.at[h, i], rz.at[h // 2, z], z_send.at[h, i], z_recv.at[h // 2, z], dev_z(to)
        )

    def z_start(h):
        for q in x2c[h]:
            q.wait_recv()
        for i in range(4):
            total = (
                tiles[h, x, i].astype(jnp.float32)
                + x2_l[h, i].astype(jnp.float32)
                + x2_r[h, i].astype(jnp.float32)
            ).astype(jnp.bfloat16)
            zs[h, i] = total
            to = 4 * (h % 2) + i

            @pl.when(z != to)
            def _():
                z_copy(h, i).start()

            @pl.when(z == to)
            def _():
                rz[h // 2, z] = total

    def z_drain(h):
        for i in range(4):

            @pl.when(z != 4 * (h % 2) + i)
            def _():
                z_copy(h, i).wait_send()

    sj = z // 4
    si = z % 4

    def panel_of(k, j):
        if k == 0:
            a, b = 2 * y + c, 2 * y + oc
        elif k == 1:
            a, b = 2 * ym + c, 2 * yp + oc
        elif k == 2:
            a, b = 2 * yp + c, 2 * ym + oc
        else:
            a, b = 2 * y2 + c, 2 * y2 + oc
        return a if j == 0 else b

    def my_panel(k):
        return panel_of(k, 0) * (1 - sj) + panel_of(k, 1) * sj

    def collocate(k):
        for zf in range(NZ):

            @pl.when(z != zf)
            def _():
                remote(
                    rz.at[k, zf], rz.at[k, zf], z_send.at[0, 0], z_recv.at[k, zf], dev_z(zf)
                ).wait_recv()

        block = jnp.sum(rz[k].astype(jnp.float32), axis=0).astype(jnp.bfloat16)
        s = my_panel(k)
        p = 4 * x + si
        same = jnp.logical_and(s == r, left_s[0, s, p] == right_s[0, s, p])
        scale = jnp.where(same, 1.0, 2.0).astype(jnp.float32)

        def one(t, carry):
            pa = meta_s[k, 2 * si, 12 + t]
            pb = meta_s[k, 2 * si + 1, 12 + t]
            for ch in range(G // CHUNK):
                cols = pl.ds(ch * CHUNK, CHUNK)
                prod = jnp.dot(block, basis[pb, :, cols], preferred_element_type=jnp.float32)
                row = jnp.sum(basis[pa, :, cols].astype(jnp.float32) * prod, axis=0, keepdims=True)
                row = row * scale
                for q in range(CHUNK // GL):
                    terms[k, t, pl.ds(ch * (CHUNK // GL) + q, 1), :] = row[:, q * GL : (q + 1) * GL]
            return carry

        lax.fori_loop(0, TOP, one, 0)
        vals = [terms[k, t] for t in range(TOP)]
        own = [meta_s[k, si, t] for t in range(TOP)]

        def place(o, carry):
            acc = jnp.zeros((GS, GL), jnp.float32)
            for t in range(TOP):
                acc = jnp.where(own[t] == o, vals[t], acc)
            send_e[k, o] = acc.astype(jnp.bfloat16)
            return carry

        lax.fori_loop(0, NX * NZ, place, 0)
        for d in E_ORDER:
            e_copy(k, d).start()
        arr[k, band] = send_e[k, band]

    def e_copy(k, d):
        zz, xx = (z + d // NX) % NZ, (x + d) % NX
        return remote(
            send_e.at[k, zz * NX + xx],
            arr.at[k, band],
            e_send.at[k],
            e_recv.at[k],
            dev_at(zz, xx),
        )

    def e_all(k):
        others = pl.ds(0, NX * NZ - 1)
        return remote(send_e.at[k, others], arr.at[k, others], e_send.at[k], e_recv.at[k], sib)

    def finish(k, acc):
        e_all(k).wait_recv()

        def one(i, acc):
            zf, xf = i // NX, i % NX
            jj = zf // 4
            ii = zf % 4
            s = panel_of(k, 0) * (1 - jj) + panel_of(k, 1) * jj
            val = arr[k, i].astype(jnp.float32)
            slot = hits[s * NX + xf, pl.ds(ii, 1), :]
            return tuple(acc[b] + jnp.where(slot == float(b), val, 0.0) for b in range(NBR))

        return lax.fori_loop(0, NX * NZ, one, acc)

    def to_sibling(src, dst, i, at):
        q = remote(src.at[halves[i]], dst.at[halves[i]], g_send.at[at], g_recv.at[at], sib)
        q.start()
        return q

    compute_tiles(coeffs, 0, panel_of(0, 0))
    x1_start(0)
    for m in m_x:
        m.wait_recv()
    m_z = []
    for d in Z_ORDER:
        to = (z + d) % NZ
        q = remote(mx, mz.at[z], m_send.at[4 + d], m_recv.at[4 + d], dev_z(to))
        q.start()
        m_z.append(q)
    mz[z] = mx[...]
    g_s.wait_recv()
    compute_tiles(b0, 1, panel_of(0, 1))
    x1_start(1)
    x2_start(0)
    g_p[0].wait_recv()
    for q in g_m:
        q.start()
    g_fs = [to_sibling(f_a, f_b, 0, 5)]
    x2_start(1)
    for q in m_z:
        q.wait_recv()
    locals_ = []
    for k in range(4):
        q = pltpu.make_async_copy(mz.at[my_panel(k), x], meta_s.at[k], l_sem.at[k])
        q.start()
        locals_.append(q)
    lane = lax.broadcasted_iota(jnp.int32, (NX * NZ, 8, 128), 2)
    every = mz[...].reshape(NX * NZ, 8, 128)
    slots = pltpu.roll(every, 128 - TOP, axis=2)
    mine = jnp.logical_and(lane < TOP, every == band)
    found = jnp.where(mine, slots + 1, 0).astype(jnp.bfloat16).reshape(NX * NZ * 8, 128)
    ones = jnp.ones((128, 128), jnp.bfloat16)
    found = jnp.dot(found, ones, preferred_element_type=jnp.float32) - 1.0
    hits[...] = found.reshape(NX * NZ, 8, 128)

    g_p[1].wait_recv()
    g_fs.append(to_sibling(f_a, f_b, 1, 6))
    compute_tiles(f_a, 2, panel_of(1, 0))
    x1_start(2)
    z_start(0)
    for q in g_fs:
        q.wait_recv()
    compute_tiles(f_b, 3, panel_of(1, 1))
    x1_start(3)
    g_m[0].wait_recv()
    g_f = [
        remote(f_a.at[v], t_a.at[v], g_send.at[7 + i], g_recv.at[7 + i], dyp)
        for i, v in enumerate(halves)
    ]
    for q in g_f:
        q.start()
    g_ms = [to_sibling(s_a, s_b, 0, 9)]
    z_start(1)
    x2_start(2)
    x2_start(3)
    for q in locals_:
        q.wait()
    loads[5].wait()

    g_m[1].wait_recv()
    g_ms.append(to_sibling(s_a, s_b, 1, 10))
    compute_tiles(s_a, 4, panel_of(2, 0))
    x1_start(4)
    z_start(2)
    for q in g_ms:
        q.wait_recv()
    compute_tiles(s_b, 5, panel_of(2, 1))
    x1_start(5)
    g_f[0].wait_recv()
    g_ts = [to_sibling(t_a, t_b, 0, 11)]
    z_start(3)
    x2_start(4)
    collocate(0)
    x2_start(5)

    g_f[1].wait_recv()
    g_ts.append(to_sibling(t_a, t_b, 1, 12))
    compute_tiles(t_a, 6, panel_of(3, 0))
    x1_start(6)
    z_start(4)
    for q in g_ts:
        q.wait_recv()
    compute_tiles(t_b, 7, panel_of(3, 1))
    x1_start(7)
    z_start(5)
    x2_start(6)
    x2_start(7)
    collocate(1)
    z_start(6)
    z_start(7)
    collocate(2)
    acc = tuple(jnp.zeros((GS, GL), jnp.float32) for _ in range(NBR))
    acc = finish(0, acc)
    acc = finish(1, acc)
    collocate(3)
    acc = finish(2, acc)
    acc = finish(3, acc)
    for b in range(NBR):
        for q in range(GS):
            out[pl.ds(b, 1), pl.ds(q * GL, GL)] = acc[b][q : q + 1, :]

    pending += [g_s] + g_p + g_m + g_fs + g_f + g_ms + g_ts + m_x + m_z
    for h in range(8):
        pending += list(x1[h]) + list(x2c[h])
    for q in pending:
        q.wait_send()
    for h in range(8):
        z_drain(h)
    for k in range(4):
        e_all(k).wait_send()


def body(coeffs, occupation, tile_left, tile_right, owners, brick_slot, patterns, basis_table):
    def place(a, at):
        return jnp.pad(a, ((0, 8 - a.shape[0]), (at, 128 - TOP - at)))

    meta = (
        place(owners, 0)
        + place(brick_slot, TOP)
        + place(jnp.transpose(patterns, (0, 2, 1)).reshape(8, TOP), 2 * TOP)
    )
    hbm = pl.BlockSpec(memory_space=pltpu.HBM)
    bf, f32 = jnp.bfloat16, jnp.float32
    panel = pltpu.VMEM((BLOCKS, BS, KD), bf)
    dma = pltpu.SemaphoreType.DMA
    out = pl.pallas_call(
        kernel,
        out_shape=jax.ShapeDtypeStruct((NBR, G), f32),
        in_specs=[hbm] * 6,
        out_specs=pl.BlockSpec(memory_space=pltpu.VMEM),
        scratch_shapes=[
            panel,
            pltpu.VMEM((1, KD), f32),
            pltpu.VMEM((4, BS, G), bf),
        ]
        + [panel] * 8
        + [
            pltpu.VMEM((8, NX, 4, BS, BS), bf),
            pltpu.VMEM((8, 2, BS, BS), bf),
            pltpu.VMEM((8, 2, BS, BS), bf),
            pltpu.VMEM((8, 4, BS, BS), bf),
            pltpu.VMEM((8, 4, BS, BS), bf),
            pltpu.VMEM((8, 4, BS, BS), bf),
            pltpu.VMEM((4, NZ, BS, BS), bf),
            pltpu.VMEM((4, TOP, GS, GL), f32),
            pltpu.VMEM((4, NX * NZ, GS, GL), bf),
            pltpu.VMEM((4, NX * NZ, GS, GL), bf),
            pltpu.VMEM((NX, 8, 128), jnp.int32),
            pltpu.VMEM((NZ, NX, 8, 128), jnp.int32),
            pltpu.VMEM((NX * NZ, 8, 128), f32),
            pltpu.SMEM((4, 8, 128), jnp.int32),
            pltpu.SMEM((1, 8, NTP), jnp.int32),
            pltpu.SMEM((1, 8, NTP), jnp.int32),
            dma((13,)),
            dma((13,)),
            dma((8, 4)),
            dma((8, 4)),
            dma((8, 4)),
            dma((4, NZ)),
            dma((4,)),
            dma((4,)),
            dma((12,)),
            dma((12,)),
            dma((4,)),
            dma((6,)),
        ],
        compiler_params=pltpu.CompilerParams(
            collective_id=0, has_side_effects=True, vmem_limit_bytes=VMEM
        ),
        cost_estimate=pl.CostEstimate(
            flops=4 * 10**9, bytes_accessed=4 * 10**6, transcendentals=0
        ),
    )(
        coeffs.reshape(BLOCKS, BS, KD),
        occupation.reshape(1, KD),
        tile_left,
        tile_right,
        meta,
        basis_table,
    )
    return out


def solution(mesh):
    return jax.shard_map(
        body,
        mesh=mesh,
        in_specs=(
            P("row", "band"),
            P("band"),
            P("row", None, None),
            P("row", None, None),
            P(("row", "band"), None),
            P(("row", "band"), None),
            P(("row", "band"), None, None),
            P(),
        ),
        out_specs=P(("row", "band"), None),
        check_vma=False,
    )
```

```python
import jax
import jax.numpy as jnp
from jax import lax
from jax.experimental import pallas as pl
from jax.experimental.pallas import tpu as pltpu
from jax.sharding import PartitionSpec as P

BS = 128
NBR = 8
TOP = 6
G = 2048
GS, GL = 16, 128
NTP = 16
BLOCKS = 8
KD = 512
NX, NY, NZ = 4, 4, 8
CHUNK = 512
Z_ORDER = (4, 3, 5, 2, 6, 1, 7)
X_ORDER = (2, 1, 3)
E_ORDER = tuple(zz * NX + xx for zz in Z_ORDER + (0,) for xx in (2, 1, 3, 0) if zz or xx)
VMEM = 62 * 2**20
MESH = pl.DeviceIdType.MESH


def kernel(
    coeffs_hbm,
    occ_hbm,
    left_hbm,
    right_hbm,
    meta_hbm,
    basis_hbm,
    out,
    coeffs,
    occ,
    basis,
    w,
    b0,
    f_a,
    f_b,
    s_a,
    s_b,
    t_a,
    t_b,
    tiles,
    x1_l,
    x1_r,
    x2_l,
    x2_r,
    zs,
    rz,
    terms,
    send_e,
    arr,
    mx,
    mz,
    hits,
    meta_s,
    left_s,
    right_s,
    g_send,
    g_recv,
    x_send,
    x_recv,
    z_send,
    z_recv,
    e_send,
    e_recv,
    m_send,
    m_recv,
    l_sem,
    i_sem,
):
    r = lax.axis_index("row")
    band = lax.axis_index("band")
    y, c = r // 2, r % 2
    z, x = band // NX, band % NX
    sg = 1 - 2 * c
    yp, ym, y2 = (y + sg + NY) % NY, (y - sg + NY) % NY, (y + 2) % NY
    oc = 1 - c
    xr, xl, x2 = (x + 1) % NX, (x + 3) % NX, (x + 2) % NX

    def dev_row(rr):
        return (rr, band)

    def dev_x(xx):
        return (r, z * NX + xx)

    def dev_at(zz, xx):
        return (r, zz * NX + xx)

    def dev_z(zz):
        return (r, zz * NX + x)

    sib = dev_row(2 * y + oc)
    dyp = dev_row(2 * yp + c)
    dym = dev_row(2 * ym + c)

    def remote(src, dst, ss, rs, dev):
        return pltpu.make_async_remote_copy(
            src_ref=src, dst_ref=dst, send_sem=ss, recv_sem=rs, device_id=dev, device_id_type=MESH
        )

    barrier = pltpu.get_barrier_semaphore()
    peers = [sib, dyp, dym]
    peers += [dev_at((z + d // NX) % NZ, (x + d) % NX) for d in range(1, NX * NZ)]
    for p in peers:
        pl.semaphore_signal(barrier, inc=1, device_id=p, device_id_type=MESH)

    loads = [
        pltpu.make_async_copy(src, dst, i_sem.at[i])
        for i, (src, dst) in enumerate(
            (
                (coeffs_hbm, coeffs),
                (occ_hbm, occ),
                (left_hbm, left_s),
                (right_hbm, right_s),
                (meta_hbm, mx.at[x]),
                (basis_hbm, basis),
            )
        )
    ]
    for q in loads:
        q.start()
    pl.semaphore_wait(barrier, len(peers))

    pending = []
    halves = (pl.ds(0, BLOCKS // 2), pl.ds(BLOCKS // 2, BLOCKS // 2))
    g_s = remote(coeffs_hbm, b0, g_send.at[0], g_recv.at[0], sib)
    g_p = [
        remote(coeffs_hbm.at[v], f_a.at[v], g_send.at[1 + i], g_recv.at[1 + i], dyp)
        for i, v in enumerate(halves)
    ]
    g_m = [
        remote(coeffs_hbm.at[v], s_a.at[v], g_send.at[3 + i], g_recv.at[3 + i], dym)
        for i, v in enumerate(halves)
    ]
    m_x = [
        remote(mx.at[x], mx.at[x], m_send.at[d], m_recv.at[d], dev_x((x + d) % NX)) for d in X_ORDER
    ]
    for q in g_p + [g_s]:
        q.start()
    for q in loads[:5]:
        q.wait()
    for q in m_x:
        q.start()
    w[...] = (coeffs[...].astype(jnp.float32) * occ[...]).astype(jnp.bfloat16)

    def compute_tiles(panel, h, s):
        def one(p, carry):
            a = w[left_s[0, s, p]]
            b = panel[right_s[0, s, p]]
            t = lax.dot_general(
                a, b, (((1,), (1,)), ((), ())), preferred_element_type=jnp.float32
            )
            tiles[h, p // 4, p % 4] = t.astype(jnp.bfloat16)
            return carry

        lax.fori_loop(0, NTP, one, 0, unroll=4)

    x1 = {}
    x2c = {}
    top, low = pl.ds(0, 2), pl.ds(2, 2)

    def x1_start(h):
        x1[h] = (
            remote(tiles.at[h, x2, top], x1_l.at[h], x_send.at[h, 0], x_recv.at[h, 0], dev_x(xr)),
            remote(tiles.at[h, x2, low], x1_r.at[h], x_send.at[h, 1], x_recv.at[h, 1], dev_x(xl)),
        )
        for q in x1[h]:
            q.start()

    def x2_start(h):
        to_r = remote(tiles.at[h, xr], x2_l.at[h], x_send.at[h, 2], x_recv.at[h, 2], dev_x(xr))
        to_l = remote(tiles.at[h, xl], x2_r.at[h], x_send.at[h, 3], x_recv.at[h, 3], dev_x(xl))
        for part, dst, got, first, second in (
            (top, xr, x1_l, x1[h][0], to_r),
            (low, xl, x1_r, x1[h][1], to_l),
        ):
            first.wait_recv()
            tiles[h, dst, part] = (
                tiles[h, dst, part].astype(jnp.float32) + got[h].astype(jnp.float32)
            ).astype(jnp.bfloat16)
            second.start()
        x2c[h] = (to_r, to_l)

    def z_copy(h, i):
        to = 2 * i + h % 2
        return remote(
            zs.at[h, i], rz.at[h // 2, z], z_send.at[h, i], z_recv.at[h // 2, z], dev_z(to)
        )

    def z_start(h):
        for q in x2c[h]:
            q.wait_recv()
        for i in range(4):
            total = (
                tiles[h, x, i].astype(jnp.float32)
                + x2_l[h, i].astype(jnp.float32)
                + x2_r[h, i].astype(jnp.float32)
            ).astype(jnp.bfloat16)
            zs[h, i] = total
            to = 2 * i + h % 2

            @pl.when(z != to)
            def _():
                z_copy(h, i).start()

            @pl.when(z == to)
            def _():
                rz[h // 2, z] = total

    def z_drain(h):
        for i in range(4):

            @pl.when(z != 2 * i + h % 2)
            def _():
                z_copy(h, i).wait_send()

    sj = z % 2
    si = z // 2

    def panel_of(k, j):
        if k == 0:
            a, b = 2 * y + c, 2 * y + oc
        elif k == 1:
            a, b = 2 * ym + c, 2 * yp + oc
        elif k == 2:
            a, b = 2 * yp + c, 2 * ym + oc
        else:
            a, b = 2 * y2 + c, 2 * y2 + oc
        return a if j == 0 else b

    def my_panel(k):
        return panel_of(k, 0) * (1 - sj) + panel_of(k, 1) * sj

    def collocate(k):
        for zf in range(NZ):

            @pl.when(z != zf)
            def _():
                remote(
                    rz.at[k, zf], rz.at[k, zf], z_send.at[0, 0], z_recv.at[k, zf], dev_z(zf)
                ).wait_recv()

        block = jnp.sum(rz[k].astype(jnp.float32), axis=0).astype(jnp.bfloat16)
        s = my_panel(k)
        p = 4 * x + si
        same = jnp.logical_and(s == r, left_s[0, s, p] == right_s[0, s, p])
        scale = jnp.where(same, 1.0, 2.0).astype(jnp.float32)

        def one(t, carry):
            pa = meta_s[k, 2 * si, 12 + t]
            pb = meta_s[k, 2 * si + 1, 12 + t]
            for ch in range(G // CHUNK):
                cols = pl.ds(ch * CHUNK, CHUNK)
                prod = jnp.dot(block, basis[pb, :, cols], preferred_element_type=jnp.float32)
                row = jnp.sum(basis[pa, :, cols].astype(jnp.float32) * prod, axis=0, keepdims=True)
                row = row * scale
                for q in range(CHUNK // GL):
                    terms[k, t, pl.ds(ch * (CHUNK // GL) + q, 1), :] = row[:, q * GL : (q + 1) * GL]
            return carry

        lax.fori_loop(0, TOP, one, 0)
        vals = [terms[k, t] for t in range(TOP)]
        own = [meta_s[k, si, t] for t in range(TOP)]

        def place(o, carry):
            acc = jnp.zeros((GS, GL), jnp.float32)
            for t in range(TOP):
                acc = jnp.where(own[t] == o, vals[t], acc)
            send_e[k, o] = acc.astype(jnp.bfloat16)
            return carry

        lax.fori_loop(0, NX * NZ, place, 0)
        for d in E_ORDER:
            e_copy(k, d).start()
        arr[k, band] = send_e[k, band]

    z_at = [lax.rem(z + d, NZ) for d in range(NZ)]
    x_at = [lax.rem(x + d, NX) for d in range(NX)]

    def e_copy(k, d):
        zz, xx = z_at[d // NX], x_at[d % NX]
        return remote(
            send_e.at[k, zz * NX + xx],
            arr.at[k, band],
            e_send.at[k],
            e_recv.at[k],
            dev_at(zz, xx),
        )

    def e_all(k):
        others = pl.ds(0, NX * NZ - 1)
        return remote(send_e.at[k, others], arr.at[k, others], e_send.at[k], e_recv.at[k], sib)

    def finish(k, acc):
        e_all(k).wait_recv()

        def one(i, acc):
            zf, xf = i // NX, i % NX
            jj = zf % 2
            ii = zf // 2
            s = panel_of(k, 0) * (1 - jj) + panel_of(k, 1) * jj
            val = arr[k, i].astype(jnp.float32)
            slot = hits[s * NX + xf, pl.ds(ii, 1), :]
            return tuple(acc[b] + jnp.where(slot == float(b), val, 0.0) for b in range(NBR))

        return lax.fori_loop(0, NX * NZ, one, acc)

    def to_sibling(src, dst, i, at):
        q = remote(src.at[halves[i]], dst.at[halves[i]], g_send.at[at], g_recv.at[at], sib)
        q.start()
        return q

    compute_tiles(coeffs, 0, panel_of(0, 0))
    x1_start(0)
    for m in m_x:
        m.wait_recv()
    m_z = []
    for d in Z_ORDER:
        to = (z + d) % NZ
        q = remote(mx, mz.at[z], m_send.at[4 + d], m_recv.at[4 + d], dev_z(to))
        q.start()
        m_z.append(q)
    mz[z] = mx[...]
    g_s.wait_recv()
    compute_tiles(b0, 1, panel_of(0, 1))
    x1_start(1)
    x2_start(0)
    g_p[0].wait_recv()
    for q in g_m:
        q.start()
    g_fs = [to_sibling(f_a, f_b, 0, 5)]
    x2_start(1)
    for q in m_z:
        q.wait_recv()
    locals_ = []
    for k in range(4):
        q = pltpu.make_async_copy(mz.at[my_panel(k), x], meta_s.at[k], l_sem.at[k])
        q.start()
        locals_.append(q)
    lane = lax.broadcasted_iota(jnp.int32, (NX * NZ, 8, 128), 2)
    every = mz[...].reshape(NX * NZ, 8, 128)
    slots = pltpu.roll(every, 128 - TOP, axis=2)
    mine = jnp.logical_and(lane < TOP, every == band)
    found = jnp.where(mine, slots + 1, 0).astype(jnp.bfloat16).reshape(NX * NZ * 8, 128)
    ones = jnp.ones((128, 128), jnp.bfloat16)
    found = jnp.dot(found, ones, preferred_element_type=jnp.float32) - 1.0
    hits[...] = found.reshape(NX * NZ, 8, 128)

    g_p[1].wait_recv()
    g_fs.append(to_sibling(f_a, f_b, 1, 6))
    compute_tiles(f_a, 2, panel_of(1, 0))
    x1_start(2)
    z_start(0)
    for q in g_fs:
        q.wait_recv()
    compute_tiles(f_b, 3, panel_of(1, 1))
    x1_start(3)
    g_m[0].wait_recv()
    g_f = [
        remote(f_a.at[v], t_a.at[v], g_send.at[7 + i], g_recv.at[7 + i], dyp)
        for i, v in enumerate(halves)
    ]
    for q in g_f:
        q.start()
    g_ms = [to_sibling(s_a, s_b, 0, 9)]
    z_start(1)
    x2_start(2)
    x2_start(3)
    for q in locals_:
        q.wait()
    loads[5].wait()

    g_m[1].wait_recv()
    g_ms.append(to_sibling(s_a, s_b, 1, 10))
    compute_tiles(s_a, 4, panel_of(2, 0))
    x1_start(4)
    z_start(2)
    for q in g_ms:
        q.wait_recv()
    compute_tiles(s_b, 5, panel_of(2, 1))
    x1_start(5)
    g_f[0].wait_recv()
    g_ts = [to_sibling(t_a, t_b, 0, 11)]
    z_start(3)
    x2_start(4)
    collocate(0)
    x2_start(5)

    g_f[1].wait_recv()
    g_ts.append(to_sibling(t_a, t_b, 1, 12))
    compute_tiles(t_a, 6, panel_of(3, 0))
    x1_start(6)
    z_start(4)
    for q in g_ts:
        q.wait_recv()
    compute_tiles(t_b, 7, panel_of(3, 1))
    x1_start(7)
    z_start(5)
    x2_start(6)
    x2_start(7)
    collocate(1)
    z_start(6)
    z_start(7)
    collocate(2)
    acc = tuple(jnp.zeros((GS, GL), jnp.float32) for _ in range(NBR))
    acc = finish(0, acc)
    acc = finish(1, acc)
    collocate(3)
    acc = finish(2, acc)
    acc = finish(3, acc)
    for b in range(NBR):
        for q in range(GS):
            out[pl.ds(b, 1), pl.ds(q * GL, GL)] = acc[b][q : q + 1, :]

    pending += [g_s] + g_p + g_m + g_fs + g_f + g_ms + g_ts + m_x + m_z
    for h in range(8):
        pending += list(x1[h]) + list(x2c[h])
    for q in pending:
        q.wait_send()
    for h in range(8):
        z_drain(h)
    for k in range(4):
        e_all(k).wait_send()


def body(coeffs, occupation, tile_left, tile_right, owners, brick_slot, patterns, basis_table):
    def place(a, at):
        return jnp.pad(a, ((0, 8 - a.shape[0]), (at, 128 - TOP - at)))

    meta = (
        place(owners, 0)
        + place(brick_slot, TOP)
        + place(jnp.transpose(patterns, (0, 2, 1)).reshape(8, TOP), 2 * TOP)
    )
    hbm = pl.BlockSpec(memory_space=pltpu.HBM)
    bf, f32 = jnp.bfloat16, jnp.float32
    panel = pltpu.VMEM((BLOCKS, BS, KD), bf)
    dma = pltpu.SemaphoreType.DMA
    out = pl.pallas_call(
        kernel,
        out_shape=jax.ShapeDtypeStruct((NBR, G), f32),
        in_specs=[hbm] * 6,
        out_specs=pl.BlockSpec(memory_space=pltpu.VMEM),
        scratch_shapes=[
            panel,
            pltpu.VMEM((1, KD), f32),
            pltpu.VMEM((4, BS, G), bf),
        ]
        + [panel] * 8
        + [
            pltpu.VMEM((8, NX, 4, BS, BS), bf),
            pltpu.VMEM((8, 2, BS, BS), bf),
            pltpu.VMEM((8, 2, BS, BS), bf),
            pltpu.VMEM((8, 4, BS, BS), bf),
            pltpu.VMEM((8, 4, BS, BS), bf),
            pltpu.VMEM((8, 4, BS, BS), bf),
            pltpu.VMEM((4, NZ, BS, BS), bf),
            pltpu.VMEM((4, TOP, GS, GL), f32),
            pltpu.VMEM((4, NX * NZ, GS, GL), bf),
            pltpu.VMEM((4, NX * NZ, GS, GL), bf),
            pltpu.VMEM((NX, 8, 128), jnp.int32),
            pltpu.VMEM((NZ, NX, 8, 128), jnp.int32),
            pltpu.VMEM((NX * NZ, 8, 128), f32),
            pltpu.SMEM((4, 8, 128), jnp.int32),
            pltpu.SMEM((1, 8, NTP), jnp.int32),
            pltpu.SMEM((1, 8, NTP), jnp.int32),
            dma((13,)),
            dma((13,)),
            dma((8, 4)),
            dma((8, 4)),
            dma((8, 4)),
            dma((4, NZ)),
            dma((4,)),
            dma((4,)),
            dma((12,)),
            dma((12,)),
            dma((4,)),
            dma((6,)),
        ],
        compiler_params=pltpu.CompilerParams(
            collective_id=0, has_side_effects=True, vmem_limit_bytes=VMEM
        ),
        cost_estimate=pl.CostEstimate(
            flops=4 * 10**9, bytes_accessed=4 * 10**6, transcendentals=0
        ),
    )(
        coeffs.reshape(BLOCKS, BS, KD),
        occupation.reshape(1, KD),
        tile_left,
        tile_right,
        meta,
        basis_table,
    )
    return out


def solution(mesh):
    return jax.shard_map(
        body,
        mesh=mesh,
        in_specs=(
            P("row", "band"),
            P("band"),
            P("row", None, None),
            P("row", None, None),
            P(("row", "band"), None),
            P(("row", "band"), None),
            P(("row", "band"), None, None),
            P(),
        ),
        out_specs=P(("row", "band"), None),
        check_vma=False,
    )
```

```python
import jax
import jax.numpy as jnp
from jax import lax
from jax.experimental import pallas as pl
from jax.experimental.pallas import tpu as pltpu
from jax.sharding import PartitionSpec as P

BS = 128
NBR = 8
TOP = 6
G = 2048
GS, GL = 16, 128
NTP = 16
BLOCKS = 8
KD = 512
NX, NY, NZ = 4, 4, 8
CHUNK = 512
Z_ORDER = (4, 3, 5, 2, 6, 1, 7)
X_ORDER = (2, 1, 3)
E_ORDER = tuple(zz * NX + xx for zz in Z_ORDER + (0,) for xx in (2, 1, 3, 0) if zz or xx)
VMEM = 62 * 2**20
MESH = pl.DeviceIdType.MESH


def kernel(
    coeffs_hbm,
    occ_hbm,
    left_hbm,
    right_hbm,
    meta_hbm,
    basis_hbm,
    out,
    coeffs,
    occ,
    basis,
    w,
    b0,
    f_a,
    f_b,
    s_a,
    s_b,
    t_a,
    t_b,
    tiles,
    x1_l,
    x1_r,
    x2_l,
    x2_r,
    zs,
    rz,
    terms,
    send_e,
    arr,
    mx,
    mz,
    hits,
    meta_s,
    left_s,
    right_s,
    g_send,
    g_recv,
    x_send,
    x_recv,
    z_send,
    z_recv,
    e_send,
    e_recv,
    m_send,
    m_recv,
    l_sem,
    i_sem,
):
    r = lax.axis_index("row")
    band = lax.axis_index("band")
    y, c = r // 2, r % 2
    z, x = band // NX, band % NX
    sg = 1 - 2 * c
    yp, ym, y2 = (y + sg + NY) % NY, (y - sg + NY) % NY, (y + 2) % NY
    oc = 1 - c
    xr, xl, x2 = (x + 1) % NX, (x + 3) % NX, (x + 2) % NX

    def dev_row(rr):
        return (rr, band)

    def dev_x(xx):
        return (r, z * NX + xx)

    def dev_at(zz, xx):
        return (r, zz * NX + xx)

    def dev_z(zz):
        return (r, zz * NX + x)

    sib = dev_row(2 * y + oc)
    dyp = dev_row(2 * yp + c)
    dym = dev_row(2 * ym + c)

    def remote(src, dst, ss, rs, dev):
        return pltpu.make_async_remote_copy(
            src_ref=src, dst_ref=dst, send_sem=ss, recv_sem=rs, device_id=dev, device_id_type=MESH
        )

    barrier = pltpu.get_barrier_semaphore()
    peers = [sib, dyp, dym]
    peers += [dev_x((x + d) % NX) for d in X_ORDER]
    peers += [dev_z((z + d) % NZ) for d in Z_ORDER]
    for p in peers:
        pl.semaphore_signal(barrier, inc=1, device_id=p, device_id_type=MESH)

    loads = [
        pltpu.make_async_copy(src, dst, i_sem.at[i])
        for i, (src, dst) in enumerate(
            (
                (coeffs_hbm, coeffs),
                (occ_hbm, occ),
                (left_hbm, left_s),
                (right_hbm, right_s),
                (meta_hbm, mx.at[x]),
                (basis_hbm, basis),
            )
        )
    ]
    for q in loads:
        q.start()
    pl.semaphore_wait(barrier, len(peers))

    pending = []
    halves = (pl.ds(0, BLOCKS // 2), pl.ds(BLOCKS // 2, BLOCKS // 2))
    g_s = remote(coeffs_hbm, b0, g_send.at[0], g_recv.at[0], sib)
    g_p = [
        remote(coeffs_hbm.at[v], f_a.at[v], g_send.at[1 + i], g_recv.at[1 + i], dyp)
        for i, v in enumerate(halves)
    ]
    g_m = [
        remote(coeffs_hbm.at[v], s_a.at[v], g_send.at[3 + i], g_recv.at[3 + i], dym)
        for i, v in enumerate(halves)
    ]
    m_x = [
        remote(mx.at[x], mx.at[x], m_send.at[d], m_recv.at[d], dev_x((x + d) % NX)) for d in X_ORDER
    ]
    for q in g_p + [g_s]:
        q.start()
    for q in loads[:5]:
        q.wait()
    for q in m_x:
        q.start()
    w[...] = (coeffs[...].astype(jnp.float32) * occ[...]).astype(jnp.bfloat16)

    def compute_tiles(panel, h, s):
        def one(p, carry):
            a = w[left_s[0, s, p]]
            b = panel[right_s[0, s, p]]
            t = lax.dot_general(
                a, b, (((1,), (1,)), ((), ())), preferred_element_type=jnp.float32
            )
            tiles[h, p // 4, p % 4] = t.astype(jnp.bfloat16)
            return carry

        lax.fori_loop(0, NTP, one, 0, unroll=4)

    x1 = {}
    x2c = {}
    top, low = pl.ds(0, 2), pl.ds(2, 2)

    def x1_start(h):
        x1[h] = (
            remote(tiles.at[h, x2, top], x1_l.at[h], x_send.at[h, 0], x_recv.at[h, 0], dev_x(xr)),
            remote(tiles.at[h, x2, low], x1_r.at[h], x_send.at[h, 1], x_recv.at[h, 1], dev_x(xl)),
        )
        for q in x1[h]:
            q.start()

    def x2_start(h):
        to_r = remote(tiles.at[h, xr], x2_l.at[h], x_send.at[h, 2], x_recv.at[h, 2], dev_x(xr))
        to_l = remote(tiles.at[h, xl], x2_r.at[h], x_send.at[h, 3], x_recv.at[h, 3], dev_x(xl))
        for part, dst, got, first, second in (
            (top, xr, x1_l, x1[h][0], to_r),
            (low, xl, x1_r, x1[h][1], to_l),
        ):
            first.wait_recv()
            tiles[h, dst, part] = (
                tiles[h, dst, part].astype(jnp.float32) + got[h].astype(jnp.float32)
            ).astype(jnp.bfloat16)
            second.start()
        x2c[h] = (to_r, to_l)

    def z_copy(h, i):
        to = 2 * i + h % 2
        return remote(
            zs.at[h, i], rz.at[h // 2, z], z_send.at[h, i], z_recv.at[h // 2, z], dev_z(to)
        )

    def z_start(h):
        for q in x2c[h]:
            q.wait_recv()
        for i in range(4):
            total = (
                tiles[h, x, i].astype(jnp.float32)
                + x2_l[h, i].astype(jnp.float32)
                + x2_r[h, i].astype(jnp.float32)
            ).astype(jnp.bfloat16)
            zs[h, i] = total
            to = 2 * i + h % 2

            @pl.when(z != to)
            def _():
                z_copy(h, i).start()

            @pl.when(z == to)
            def _():
                rz[h // 2, z] = total

    def z_drain(h):
        for i in range(4):

            @pl.when(z != 2 * i + h % 2)
            def _():
                z_copy(h, i).wait_send()

    sj = z % 2
    si = z // 2

    def panel_of(k, j):
        if k == 0:
            a, b = 2 * y + c, 2 * y + oc
        elif k == 1:
            a, b = 2 * ym + c, 2 * yp + oc
        elif k == 2:
            a, b = 2 * yp + c, 2 * ym + oc
        else:
            a, b = 2 * y2 + c, 2 * y2 + oc
        return a if j == 0 else b

    def my_panel(k):
        return panel_of(k, 0) * (1 - sj) + panel_of(k, 1) * sj

    def collocate(k):
        for zf in range(NZ):

            @pl.when(z != zf)
            def _():
                remote(
                    rz.at[k, zf], rz.at[k, zf], z_send.at[0, 0], z_recv.at[k, zf], dev_z(zf)
                ).wait_recv()

        block = jnp.sum(rz[k].astype(jnp.float32), axis=0).astype(jnp.bfloat16)
        s = my_panel(k)
        p = 4 * x + si
        same = jnp.logical_and(s == r, left_s[0, s, p] == right_s[0, s, p])
        scale = jnp.where(same, 1.0, 2.0).astype(jnp.float32)

        def one(t, carry):
            pa = meta_s[k, 2 * si, 12 + t]
            pb = meta_s[k, 2 * si + 1, 12 + t]
            for ch in range(G // CHUNK):
                cols = pl.ds(ch * CHUNK, CHUNK)
                prod = jnp.dot(block, basis[pb, :, cols], preferred_element_type=jnp.float32)
                row = jnp.sum(basis[pa, :, cols].astype(jnp.float32) * prod, axis=0, keepdims=True)
                row = row * scale
                for q in range(CHUNK // GL):
                    terms[k, t, pl.ds(ch * (CHUNK // GL) + q, 1), :] = row[:, q * GL : (q + 1) * GL]
            return carry

        lax.fori_loop(0, TOP, one, 0, unroll=True)
        vals = [terms[k, t] for t in range(TOP)]
        own = [meta_s[k, si, t] for t in range(TOP)]

        def place(o, carry):
            acc = jnp.zeros((GS, GL), jnp.float32)
            for t in range(TOP):
                acc = jnp.where(own[t] == o, vals[t], acc)
            send_e[k, o] = acc.astype(jnp.bfloat16)
            return carry

        lax.fori_loop(0, NX * NZ, place, 0, unroll=4)
        for d in E_ORDER:
            e_copy(k, d).start()
        arr[k, band] = send_e[k, band]

    z_at = [lax.rem(z + d, NZ) for d in range(NZ)]
    x_at = [lax.rem(x + d, NX) for d in range(NX)]

    def e_copy(k, d):
        zz, xx = z_at[d // NX], x_at[d % NX]
        return remote(
            send_e.at[k, zz * NX + xx],
            arr.at[k, band],
            e_send.at[k],
            e_recv.at[k],
            dev_at(zz, xx),
        )

    def e_all(k):
        others = pl.ds(0, NX * NZ - 1)
        return remote(send_e.at[k, others], arr.at[k, others], e_send.at[k], e_recv.at[k], sib)

    def finish(k, acc):
        e_all(k).wait_recv()

        def one(i, acc):
            zf, xf = i // NX, i % NX
            jj = zf % 2
            ii = zf // 2
            s = panel_of(k, 0) * (1 - jj) + panel_of(k, 1) * jj
            val = arr[k, i].astype(jnp.float32)
            slot = hits[s * NX + xf, pl.ds(ii, 1), :]
            return tuple(acc[b] + jnp.where(slot == float(b), val, 0.0) for b in range(NBR))

        return lax.fori_loop(0, NX * NZ, one, acc, unroll=4)

    def to_sibling(src, dst, i, at):
        q = remote(src.at[halves[i]], dst.at[halves[i]], g_send.at[at], g_recv.at[at], sib)
        q.start()
        return q

    compute_tiles(coeffs, 0, panel_of(0, 0))
    x1_start(0)
    for m in m_x:
        m.wait_recv()
    m_z = []
    for d in Z_ORDER:
        to = (z + d) % NZ
        q = remote(mx, mz.at[z], m_send.at[4 + d], m_recv.at[4 + d], dev_z(to))
        q.start()
        m_z.append(q)
    mz[z] = mx[...]
    g_s.wait_recv()
    compute_tiles(b0, 1, panel_of(0, 1))
    x1_start(1)
    x2_start(0)
    g_p[0].wait_recv()
    for q in g_m:
        q.start()
    g_fs = [to_sibling(f_a, f_b, 0, 5)]
    x2_start(1)
    for q in m_z:
        q.wait_recv()
    locals_ = []
    for k in range(4):
        q = pltpu.make_async_copy(mz.at[my_panel(k), x], meta_s.at[k], l_sem.at[k])
        q.start()
        locals_.append(q)
    lane = lax.broadcasted_iota(jnp.int32, (NX * NZ, 8, 128), 2)
    every = mz[...].reshape(NX * NZ, 8, 128)
    slots = pltpu.roll(every, 128 - TOP, axis=2)
    mine = jnp.logical_and(lane < TOP, every == band)
    found = jnp.where(mine, slots + 1, 0).astype(jnp.bfloat16).reshape(NX * NZ * 8, 128)
    ones = jnp.ones((128, 128), jnp.bfloat16)
    found = jnp.dot(found, ones, preferred_element_type=jnp.float32) - 1.0
    hits[...] = found.reshape(NX * NZ, 8, 128)

    g_p[1].wait_recv()
    g_fs.append(to_sibling(f_a, f_b, 1, 6))
    compute_tiles(f_a, 2, panel_of(1, 0))
    x1_start(2)
    z_start(0)
    for q in g_fs:
        q.wait_recv()
    compute_tiles(f_b, 3, panel_of(1, 1))
    x1_start(3)
    g_m[0].wait_recv()
    g_f = [
        remote(f_a.at[v], t_a.at[v], g_send.at[7 + i], g_recv.at[7 + i], dyp)
        for i, v in enumerate(halves)
    ]
    for q in g_f:
        q.start()
    g_ms = [to_sibling(s_a, s_b, 0, 9)]
    z_start(1)
    x2_start(2)
    x2_start(3)
    for q in locals_:
        q.wait()
    loads[5].wait()

    g_m[1].wait_recv()
    g_ms.append(to_sibling(s_a, s_b, 1, 10))
    compute_tiles(s_a, 4, panel_of(2, 0))
    x1_start(4)
    z_start(2)
    for q in g_ms:
        q.wait_recv()
    compute_tiles(s_b, 5, panel_of(2, 1))
    x1_start(5)
    g_f[0].wait_recv()
    g_ts = [to_sibling(t_a, t_b, 0, 11)]
    z_start(3)
    x2_start(4)
    collocate(0)
    x2_start(5)

    g_f[1].wait_recv()
    g_ts.append(to_sibling(t_a, t_b, 1, 12))
    compute_tiles(t_a, 6, panel_of(3, 0))
    x1_start(6)
    z_start(4)
    for q in g_ts:
        q.wait_recv()
    compute_tiles(t_b, 7, panel_of(3, 1))
    x1_start(7)
    z_start(5)
    x2_start(6)
    x2_start(7)
    collocate(1)
    z_start(6)
    z_start(7)
    collocate(2)
    acc = tuple(jnp.zeros((GS, GL), jnp.float32) for _ in range(NBR))
    acc = finish(0, acc)
    acc = finish(1, acc)
    collocate(3)
    acc = finish(2, acc)
    acc = finish(3, acc)
    for b in range(NBR):
        for q in range(GS):
            out[pl.ds(b, 1), pl.ds(q * GL, GL)] = acc[b][q : q + 1, :]

    pending += [g_s] + g_p + g_m + g_fs + g_f + g_ms + g_ts + m_x + m_z
    for h in range(8):
        pending += list(x1[h]) + list(x2c[h])
    for q in pending:
        q.wait_send()
    for h in range(8):
        z_drain(h)
    for k in range(4):
        e_all(k).wait_send()


def body(coeffs, occupation, tile_left, tile_right, owners, brick_slot, patterns, basis_table):
    def place(a, at):
        return jnp.pad(a, ((0, 8 - a.shape[0]), (at, 128 - TOP - at)))

    meta = (
        place(owners, 0)
        + place(brick_slot, TOP)
        + place(jnp.transpose(patterns, (0, 2, 1)).reshape(8, TOP), 2 * TOP)
    )
    hbm = pl.BlockSpec(memory_space=pltpu.HBM)
    bf, f32 = jnp.bfloat16, jnp.float32
    panel = pltpu.VMEM((BLOCKS, BS, KD), bf)
    dma = pltpu.SemaphoreType.DMA
    out = pl.pallas_call(
        kernel,
        out_shape=jax.ShapeDtypeStruct((NBR, G), f32),
        in_specs=[hbm] * 6,
        out_specs=pl.BlockSpec(memory_space=pltpu.VMEM),
        scratch_shapes=[
            panel,
            pltpu.VMEM((1, KD), f32),
            pltpu.VMEM((4, BS, G), bf),
        ]
        + [panel] * 8
        + [
            pltpu.VMEM((8, NX, 4, BS, BS), bf),
            pltpu.VMEM((8, 2, BS, BS), bf),
            pltpu.VMEM((8, 2, BS, BS), bf),
            pltpu.VMEM((8, 4, BS, BS), bf),
            pltpu.VMEM((8, 4, BS, BS), bf),
            pltpu.VMEM((8, 4, BS, BS), bf),
            pltpu.VMEM((4, NZ, BS, BS), bf),
            pltpu.VMEM((4, TOP, GS, GL), f32),
            pltpu.VMEM((4, NX * NZ, GS, GL), bf),
            pltpu.VMEM((4, NX * NZ, GS, GL), bf),
            pltpu.VMEM((NX, 8, 128), jnp.int32),
            pltpu.VMEM((NZ, NX, 8, 128), jnp.int32),
            pltpu.VMEM((NX * NZ, 8, 128), f32),
            pltpu.SMEM((4, 8, 128), jnp.int32),
            pltpu.SMEM((1, 8, NTP), jnp.int32),
            pltpu.SMEM((1, 8, NTP), jnp.int32),
            dma((13,)),
            dma((13,)),
            dma((8, 4)),
            dma((8, 4)),
            dma((8, 4)),
            dma((4, NZ)),
            dma((4,)),
            dma((4,)),
            dma((12,)),
            dma((12,)),
            dma((4,)),
            dma((6,)),
        ],
        compiler_params=pltpu.CompilerParams(
            collective_id=0, has_side_effects=True, vmem_limit_bytes=VMEM
        ),
        cost_estimate=pl.CostEstimate(
            flops=4 * 10**9, bytes_accessed=4 * 10**6, transcendentals=0
        ),
    )(
        coeffs.reshape(BLOCKS, BS, KD),
        occupation.reshape(1, KD),
        tile_left,
        tile_right,
        meta,
        basis_table,
    )
    return out


def solution(mesh):
    return jax.shard_map(
        body,
        mesh=mesh,
        in_specs=(
            P("row", "band"),
            P("band"),
            P("row", None, None),
            P("row", None, None),
            P(("row", "band"), None),
            P(("row", "band"), None),
            P(("row", "band"), None, None),
            P(),
        ),
        out_specs=P(("row", "band"), None),
        check_vma=False,
    )
```

```python
import jax
import jax.numpy as jnp
from jax import lax
from jax.experimental import pallas as pl
from jax.experimental.pallas import tpu as pltpu
from jax.sharding import PartitionSpec as P

BS = 128
NBR = 8
TOP = 6
G = 2048
GS, GL = 16, 128
NTP = 16
BLOCKS = 8
KD = 512
NX, NY, NZ = 4, 4, 8
CHUNK = 512
Z_ORDER = (4, 3, 5, 2, 6, 1, 7)
X_ORDER = (2, 1, 3)
E_ORDER = tuple(zz * NX + xx for zz in Z_ORDER + (0,) for xx in (2, 1, 3, 0) if zz or xx)
VMEM = 62 * 2**20
MESH = pl.DeviceIdType.MESH


def kernel(
    coeffs_hbm,
    occ_hbm,
    left_hbm,
    right_hbm,
    owners_hbm,
    slots_hbm,
    patterns_hbm,
    basis_hbm,
    out,
    coeffs,
    occ,
    basis,
    w,
    b0,
    f_a,
    f_b,
    s_a,
    s_b,
    t_a,
    t_b,
    tiles,
    x1_l,
    x1_r,
    x2_l,
    x2_r,
    zs,
    rz,
    terms,
    send_e,
    arr,
    owners_v,
    slots_v,
    patterns_v,
    mz,
    mall,
    hits,
    meta_s,
    left_s,
    right_s,
    g_send,
    g_recv,
    x_send,
    x_recv,
    z_send,
    z_recv,
    e_send,
    e_recv,
    m_send,
    m_recv,
    l_sem,
    i_sem,
):
    r = lax.axis_index("row")
    band = lax.axis_index("band")
    y, c = r // 2, r % 2
    z, x = band // NX, band % NX
    sg = 1 - 2 * c
    yp, ym, y2 = (y + sg + NY) % NY, (y - sg + NY) % NY, (y + 2) % NY
    oc = 1 - c
    xr, xl, x2 = (x + 1) % NX, (x + 3) % NX, (x + 2) % NX

    zr, zl = (z + 1) % NZ, (z + NZ - 1) % NZ

    def dev_row(rr):
        return (rr, band)

    def dev_x(xx):
        return (r, z * NX + xx)

    def dev_at(zz, xx):
        return (r, zz * NX + xx)

    def dev_z(zz):
        return (r, zz * NX + x)

    sib = dev_row(2 * y + oc)
    dyp = dev_row(2 * yp + c)
    dym = dev_row(2 * ym + c)

    def remote(src, dst, ss, rs, dev):
        return pltpu.make_async_remote_copy(
            src_ref=src, dst_ref=dst, send_sem=ss, recv_sem=rs, device_id=dev, device_id_type=MESH
        )

    barrier = pltpu.get_barrier_semaphore()
    peers = [sib, dyp, dym]
    peers += [dev_x(xr), dev_x(xl), dev_z(zr), dev_z(zl)]
    for p in peers:
        pl.semaphore_signal(barrier, inc=1, device_id=p, device_id_type=MESH)

    loads = [
        pltpu.make_async_copy(src, dst, i_sem.at[i])
        for i, (src, dst) in enumerate(
            (
                (coeffs_hbm, coeffs),
                (occ_hbm, occ),
                (left_hbm, left_s),
                (right_hbm, right_s),
                (owners_hbm, owners_v),
                (slots_hbm, slots_v),
                (patterns_hbm, patterns_v),
                (basis_hbm, basis),
            )
        )
    ]
    for q in loads:
        q.start()
    pl.semaphore_wait(barrier, len(peers))

    pending = []
    halves = (pl.ds(0, BLOCKS // 2), pl.ds(BLOCKS // 2, BLOCKS // 2))
    g_s = remote(coeffs_hbm, b0, g_send.at[0], g_recv.at[0], sib)
    g_p = [
        remote(coeffs_hbm.at[v], f_a.at[v], g_send.at[1 + i], g_recv.at[1 + i], dyp)
        for i, v in enumerate(halves)
    ]
    g_m = [
        remote(coeffs_hbm.at[v], s_a.at[v], g_send.at[3 + i], g_recv.at[3 + i], dym)
        for i, v in enumerate(halves)
    ]
    for q in g_p + [g_s]:
        q.start()
    for q in loads[:7]:
        q.wait()
    mz[z] = jnp.zeros((2, 8, 128), jnp.int32)
    mz[z, 0, pl.ds(0, 4), pl.ds(0, TOP)] = owners_v[...]
    mz[z, 0, pl.ds(4, 4), pl.ds(0, TOP)] = slots_v[...]
    mz[z, 1, :, pl.ds(0, TOP)] = patterns_v[...]

    def meta_z(step):
        at = (z + NZ - step) % NZ
        to = [remote(mz.at[at], mz.at[at], m_send.at[step], m_recv.at[step], dev_z(zr))]
        if step < 3:
            at = (z + step) % NZ
            i = 4 + step
            to.append(remote(mz.at[at], mz.at[at], m_send.at[i], m_recv.at[i], dev_z(zl)))
        for q in to:
            q.start()
        return to

    m_z = [meta_z(0)]
    w[...] = (coeffs[...].astype(jnp.float32) * occ[...]).astype(jnp.bfloat16)

    def compute_tiles(panel, h, s):
        def one(p, carry):
            a = w[left_s[0, s, p]]
            b = panel[right_s[0, s, p]]
            t = lax.dot_general(
                a, b, (((1,), (1,)), ((), ())), preferred_element_type=jnp.float32
            )
            tiles[h, p // 4, p % 4] = t.astype(jnp.bfloat16)
            return carry

        lax.fori_loop(0, NTP, one, 0, unroll=4)

    x1 = {}
    x2c = {}
    top, low = pl.ds(0, 2), pl.ds(2, 2)

    def x1_start(h):
        x1[h] = (
            remote(tiles.at[h, x2, top], x1_l.at[h], x_send.at[h, 0], x_recv.at[h, 0], dev_x(xr)),
            remote(tiles.at[h, x2, low], x1_r.at[h], x_send.at[h, 1], x_recv.at[h, 1], dev_x(xl)),
        )
        for q in x1[h]:
            q.start()

    def x2_start(h):
        to_r = remote(tiles.at[h, xr], x2_l.at[h], x_send.at[h, 2], x_recv.at[h, 2], dev_x(xr))
        to_l = remote(tiles.at[h, xl], x2_r.at[h], x_send.at[h, 3], x_recv.at[h, 3], dev_x(xl))
        for part, dst, got, first, second in (
            (top, xr, x1_l, x1[h][0], to_r),
            (low, xl, x1_r, x1[h][1], to_l),
        ):
            first.wait_recv()
            tiles[h, dst, part] = (
                tiles[h, dst, part].astype(jnp.float32) + got[h].astype(jnp.float32)
            ).astype(jnp.bfloat16)
            second.start()
        x2c[h] = (to_r, to_l)

    def z_copy(h, i):
        to = 2 * i + h % 2
        return remote(
            zs.at[h, i], rz.at[h // 2, z], z_send.at[h, i], z_recv.at[h // 2, z], dev_z(to)
        )

    def z_start(h):
        for q in x2c[h]:
            q.wait_recv()
        for i in range(4):
            total = (
                tiles[h, x, i].astype(jnp.float32)
                + x2_l[h, i].astype(jnp.float32)
                + x2_r[h, i].astype(jnp.float32)
            ).astype(jnp.bfloat16)
            zs[h, i] = total
            to = 2 * i + h % 2

            @pl.when(z != to)
            def _():
                z_copy(h, i).start()

            @pl.when(z == to)
            def _():
                rz[h // 2, z] = total

    def z_drain(h):
        for i in range(4):

            @pl.when(z != 2 * i + h % 2)
            def _():
                z_copy(h, i).wait_send()

    sj = z % 2
    si = z // 2

    def panel_of(k, j):
        if k == 0:
            a, b = 2 * y + c, 2 * y + oc
        elif k == 1:
            a, b = 2 * ym + c, 2 * yp + oc
        elif k == 2:
            a, b = 2 * yp + c, 2 * ym + oc
        else:
            a, b = 2 * y2 + c, 2 * y2 + oc
        return a if j == 0 else b

    def my_panel(k):
        return panel_of(k, 0) * (1 - sj) + panel_of(k, 1) * sj

    def collocate(k):
        for zf in range(NZ):

            @pl.when(z != zf)
            def _():
                remote(
                    rz.at[k, zf], rz.at[k, zf], z_send.at[0, 0], z_recv.at[k, zf], dev_z(zf)
                ).wait_recv()

        block = jnp.sum(rz[k].astype(jnp.float32), axis=0).astype(jnp.bfloat16)
        s = my_panel(k)
        p = 4 * x + si
        same = jnp.logical_and(s == r, left_s[0, s, p] == right_s[0, s, p])
        scale = jnp.where(same, 1.0, 2.0).astype(jnp.float32)

        def one(t, carry):
            pa = meta_s[k, 1, 2 * si, t]
            pb = meta_s[k, 1, 2 * si + 1, t]
            for ch in range(G // CHUNK):
                cols = pl.ds(ch * CHUNK, CHUNK)
                prod = jnp.dot(block, basis[pb, :, cols], preferred_element_type=jnp.float32)
                row = jnp.sum(basis[pa, :, cols].astype(jnp.float32) * prod, axis=0, keepdims=True)
                row = row * scale
                for q in range(CHUNK // GL):
                    terms[k, t, pl.ds(ch * (CHUNK // GL) + q, 1), :] = row[:, q * GL : (q + 1) * GL]
            return carry

        lax.fori_loop(0, TOP, one, 0, unroll=True)
        vals = [terms[k, t] for t in range(TOP)]
        own = [meta_s[k, 0, si, t] for t in range(TOP)]

        def place(o, carry):
            acc = jnp.zeros((GS, GL), jnp.float32)
            for t in range(TOP):
                acc = jnp.where(own[t] == o, vals[t], acc)
            send_e[k, o] = acc.astype(jnp.bfloat16)
            return carry

        lax.fori_loop(0, NX * NZ, place, 0, unroll=4)
        for d in E_ORDER:
            e_copy(k, d).start()
        arr[k, band] = send_e[k, band]

    z_at = [lax.rem(z + d, NZ) for d in range(NZ)]
    x_at = [lax.rem(x + d, NX) for d in range(NX)]

    def e_copy(k, d):
        zz, xx = z_at[d // NX], x_at[d % NX]
        return remote(
            send_e.at[k, zz * NX + xx],
            arr.at[k, band],
            e_send.at[k],
            e_recv.at[k],
            dev_at(zz, xx),
        )

    def e_all(k):
        others = pl.ds(0, NX * NZ - 1)
        return remote(send_e.at[k, others], arr.at[k, others], e_send.at[k], e_recv.at[k], sib)

    def finish(k, acc):
        e_all(k).wait_recv()

        def one(i, acc):
            zf, xf = i // NX, i % NX
            jj = zf % 2
            ii = zf // 2
            s = panel_of(k, 0) * (1 - jj) + panel_of(k, 1) * jj
            val = arr[k, i].astype(jnp.float32)
            slot = hits[xf * NZ + s, pl.ds(ii, 1), :]
            return tuple(acc[b] + jnp.where(slot == float(b), val, 0.0) for b in range(NBR))

        return lax.fori_loop(0, NX * NZ, one, acc, unroll=4)

    pieces = halves[:1] + (pl.ds(4, 2), pl.ds(6, 2))

    def to_sibling(src, dst, v, at):
        q = remote(src.at[v], dst.at[v], g_send.at[at], g_recv.at[at], sib)
        q.start()
        return q

    compute_tiles(coeffs, 0, panel_of(0, 0))
    x1_start(0)
    g_s.wait_recv()
    compute_tiles(b0, 1, panel_of(0, 1))
    x1_start(1)

    def next_meta(step):
        for q in m_z[step - 1]:
            q.wait_recv()
        if step < 4:
            m_z.append(meta_z(step))

    next_meta(1)
    x2_start(0)
    g_p[0].wait_recv()
    for q in g_m:
        q.start()
    g_fs = [to_sibling(f_a, f_b, halves[0], 5)]
    next_meta(2)
    x2_start(1)
    next_meta(3)

    g_p[1].wait_recv()
    g_fs.append(to_sibling(f_a, f_b, halves[1], 6))
    compute_tiles(f_a, 2, panel_of(1, 0))
    x1_start(2)
    next_meta(4)
    locals_ = []
    for k in range(4):
        q = pltpu.make_async_copy(mz.at[my_panel(k)], meta_s.at[k], l_sem.at[k])
        q.start()
        locals_.append(q)
    mall[x] = mz[:, 0]
    m_x = [
        remote(mall.at[x], mall.at[x], m_send.at[7 + i], m_recv.at[7 + i], dev_x(to))
        for i, to in enumerate((xr, xl))
    ]
    for q in m_x:
        q.start()
    z_start(0)
    for q in g_fs:
        q.wait_recv()
    compute_tiles(f_b, 3, panel_of(1, 1))
    x1_start(3)
    g_m[0].wait_recv()
    g_f = [
        remote(f_a.at[v], t_a.at[v], g_send.at[7 + i], g_recv.at[7 + i], dyp)
        for i, v in enumerate(pieces)
    ]
    for q in g_f:
        q.start()
    g_ms = [to_sibling(s_a, s_b, halves[0], 10)]
    z_start(1)
    x2_start(2)
    x2_start(3)
    for q in m_x:
        q.wait_recv()
    m_x.append(remote(mall.at[xl], mall.at[xl], m_send.at[9], m_recv.at[9], dev_x(xr)))
    m_x[2].start()
    for q in locals_:
        q.wait()
    loads[7].wait()

    g_m[1].wait_recv()
    g_ms.append(to_sibling(s_a, s_b, halves[1], 11))
    compute_tiles(s_a, 4, panel_of(2, 0))
    x1_start(4)
    z_start(2)
    for q in g_ms:
        q.wait_recv()
    compute_tiles(s_b, 5, panel_of(2, 1))
    x1_start(5)
    g_f[0].wait_recv()
    g_ts = [to_sibling(t_a, t_b, pieces[0], 12)]
    z_start(3)
    x2_start(4)
    collocate(0)
    x2_start(5)
    m_x[2].wait_recv()
    lane = lax.broadcasted_iota(jnp.int32, (NX * NZ, 8, 128), 2)
    every = mall[...].reshape(NX * NZ, 8, 128)
    slots = pltpu.roll(every, 4, axis=1)
    mine = jnp.logical_and(lane < TOP, every == band)
    found = jnp.where(mine, slots + 1, 0).astype(jnp.bfloat16).reshape(NX * NZ * 8, 128)
    ones = jnp.ones((128, 128), jnp.bfloat16)
    found = jnp.dot(found, ones, preferred_element_type=jnp.float32) - 1.0
    hits[...] = found.reshape(NX * NZ, 8, 128)

    for i in (1, 2):
        g_f[i].wait_recv()
        g_ts.append(to_sibling(t_a, t_b, pieces[i], 12 + i))
    compute_tiles(t_a, 6, panel_of(3, 0))
    x1_start(6)
    z_start(4)
    for q in g_ts:
        q.wait_recv()
    compute_tiles(t_b, 7, panel_of(3, 1))
    x1_start(7)
    z_start(5)
    x2_start(6)
    x2_start(7)
    collocate(1)
    z_start(6)
    z_start(7)
    collocate(2)
    acc = tuple(jnp.zeros((GS, GL), jnp.float32) for _ in range(NBR))
    acc = finish(0, acc)
    acc = finish(1, acc)
    collocate(3)
    acc = finish(2, acc)
    acc = finish(3, acc)
    for b in range(NBR):
        for q in range(GS):
            out[pl.ds(b, 1), pl.ds(q * GL, GL)] = acc[b][q : q + 1, :]

    pending += [g_s] + g_p + g_m + g_fs + g_f + g_ms + g_ts + m_x + sum(m_z, [])
    for h in range(8):
        pending += list(x1[h]) + list(x2c[h])
    for q in pending:
        q.wait_send()
    for h in range(8):
        z_drain(h)
    for k in range(4):
        e_all(k).wait_send()


def body(coeffs, occupation, tile_left, tile_right, owners, brick_slot, patterns, basis_table):
    hbm = pl.BlockSpec(memory_space=pltpu.HBM)
    bf, f32 = jnp.bfloat16, jnp.float32
    panel = pltpu.VMEM((BLOCKS, BS, KD), bf)
    dma = pltpu.SemaphoreType.DMA
    out = pl.pallas_call(
        kernel,
        out_shape=jax.ShapeDtypeStruct((NBR, G), f32),
        in_specs=[hbm] * 8,
        out_specs=pl.BlockSpec(memory_space=pltpu.VMEM),
        scratch_shapes=[
            panel,
            pltpu.VMEM((1, KD), f32),
            pltpu.VMEM((4, BS, G), bf),
        ]
        + [panel] * 8
        + [
            pltpu.VMEM((8, NX, 4, BS, BS), bf),
            pltpu.VMEM((8, 2, BS, BS), bf),
            pltpu.VMEM((8, 2, BS, BS), bf),
            pltpu.VMEM((8, 4, BS, BS), bf),
            pltpu.VMEM((8, 4, BS, BS), bf),
            pltpu.VMEM((8, 4, BS, BS), bf),
            pltpu.VMEM((4, NZ, BS, BS), bf),
            pltpu.VMEM((4, TOP, GS, GL), f32),
            pltpu.VMEM((4, NX * NZ, GS, GL), bf),
            pltpu.VMEM((4, NX * NZ, GS, GL), bf),
            pltpu.VMEM((4, TOP), jnp.int32),
            pltpu.VMEM((4, TOP), jnp.int32),
            pltpu.VMEM((8, TOP), jnp.int32),
            pltpu.VMEM((NZ, 2, 8, 128), jnp.int32),
            pltpu.VMEM((NX, NZ, 8, 128), jnp.int32),
            pltpu.VMEM((NX * NZ, 8, 128), f32),
            pltpu.SMEM((4, 2, 8, 128), jnp.int32),
            pltpu.SMEM((1, 8, NTP), jnp.int32),
            pltpu.SMEM((1, 8, NTP), jnp.int32),
            dma((15,)),
            dma((15,)),
            dma((8, 4)),
            dma((8, 4)),
            dma((8, 4)),
            dma((4, NZ)),
            dma((4,)),
            dma((4,)),
            dma((10,)),
            dma((10,)),
            dma((4,)),
            dma((8,)),
        ],
        compiler_params=pltpu.CompilerParams(
            collective_id=0, has_side_effects=True, vmem_limit_bytes=VMEM
        ),
        cost_estimate=pl.CostEstimate(
            flops=4 * 10**9, bytes_accessed=4 * 10**6, transcendentals=0
        ),
    )(
        coeffs.reshape(BLOCKS, BS, KD),
        occupation.reshape(1, KD),
        tile_left,
        tile_right,
        owners,
        brick_slot,
        jnp.transpose(patterns, (0, 2, 1)).reshape(8, TOP),
        basis_table,
    )
    return out


def solution(mesh):
    return jax.shard_map(
        body,
        mesh=mesh,
        in_specs=(
            P("row", "band"),
            P("band"),
            P("row", None, None),
            P("row", None, None),
            P(("row", "band"), None),
            P(("row", "band"), None),
            P(("row", "band"), None, None),
            P(),
        ),
        out_specs=P(("row", "band"), None),
        check_vma=False,
    )
```

```python
import jax
import jax.numpy as jnp
from jax import lax
from jax.experimental import pallas as pl
from jax.experimental.pallas import tpu as pltpu
from jax.sharding import PartitionSpec as P

BS = 128
NBR = 8
TOP = 6
G = 2048
GS, GL = 16, 128
NTP = 16
BLOCKS = 8
KD = 512
NX, NY, NZ = 4, 4, 8
CHUNK = 512
Z_ORDER = (4, 3, 5, 2, 6, 1, 7)
X_ORDER = (2, 1, 3)
E_ORDER = tuple(zz * NX + xx for zz in Z_ORDER + (0,) for xx in (2, 1, 3, 0) if zz or xx)
VMEM = 62 * 2**20
MESH = pl.DeviceIdType.MESH


def kernel(
    coeffs_hbm,
    occ_hbm,
    left_hbm,
    right_hbm,
    owners_hbm,
    slots_hbm,
    patterns_hbm,
    basis_hbm,
    out,
    coeffs,
    occ,
    basis,
    w,
    b0,
    f_a,
    f_b,
    s_a,
    s_b,
    t_a,
    t_b,
    tiles,
    x1_l,
    x1_r,
    x2_l,
    x2_r,
    zs,
    rz,
    terms,
    send_e,
    arr,
    owners_v,
    slots_v,
    patterns_v,
    mz,
    mall,
    hits,
    meta_s,
    left_s,
    right_s,
    g_send,
    g_recv,
    x_send,
    x_recv,
    z_send,
    z_recv,
    e_send,
    e_recv,
    m_send,
    m_recv,
    l_sem,
    i_sem,
):
    r = lax.axis_index("row")
    band = lax.axis_index("band")
    y, c = r // 2, r % 2
    z, x = band // NX, band % NX
    sg = 1 - 2 * c
    yp, ym, y2 = (y + sg + NY) % NY, (y - sg + NY) % NY, (y + 2) % NY
    oc = 1 - c
    xr, xl, x2 = (x + 1) % NX, (x + 3) % NX, (x + 2) % NX

    zr, zl = (z + 1) % NZ, (z + NZ - 1) % NZ

    def dev_row(rr):
        return (rr, band)

    def dev_x(xx):
        return (r, z * NX + xx)

    def dev_at(zz, xx):
        return (r, zz * NX + xx)

    def dev_z(zz):
        return (r, zz * NX + x)

    sib = dev_row(2 * y + oc)
    dyp = dev_row(2 * yp + c)
    dym = dev_row(2 * ym + c)

    def remote(src, dst, ss, rs, dev):
        return pltpu.make_async_remote_copy(
            src_ref=src, dst_ref=dst, send_sem=ss, recv_sem=rs, device_id=dev, device_id_type=MESH
        )

    barrier = pltpu.get_barrier_semaphore()
    peers = [sib, dyp, dym]
    peers += [dev_x(xr), dev_x(xl), dev_z(zr), dev_z(zl)]
    for p in peers:
        pl.semaphore_signal(barrier, inc=1, device_id=p, device_id_type=MESH)

    loads = [
        pltpu.make_async_copy(src, dst, i_sem.at[i])
        for i, (src, dst) in enumerate(
            (
                (coeffs_hbm, coeffs),
                (occ_hbm, occ),
                (left_hbm, left_s),
                (right_hbm, right_s),
                (owners_hbm, owners_v),
                (slots_hbm, slots_v),
                (patterns_hbm, patterns_v),
                (basis_hbm, basis),
            )
        )
    ]
    for q in loads:
        q.start()
    pl.semaphore_wait(barrier, len(peers))

    pending = []
    halves = (pl.ds(0, BLOCKS // 2), pl.ds(BLOCKS // 2, BLOCKS // 2))
    g_s = remote(coeffs_hbm, b0, g_send.at[0], g_recv.at[0], sib)
    g_p = [
        remote(coeffs_hbm.at[v], f_a.at[v], g_send.at[1 + i], g_recv.at[1 + i], dyp)
        for i, v in enumerate(halves)
    ]
    g_m = [
        remote(coeffs_hbm.at[v], s_a.at[v], g_send.at[3 + i], g_recv.at[3 + i], dym)
        for i, v in enumerate(halves)
    ]
    for q in g_p + [g_s]:
        q.start()
    for q in loads[:7]:
        q.wait()
    mz[z] = jnp.zeros((2, 8, 128), jnp.int32)
    mz[z, 0, pl.ds(0, 4), pl.ds(0, TOP)] = owners_v[...]
    mz[z, 0, pl.ds(4, 4), pl.ds(0, TOP)] = slots_v[...]
    mz[z, 1, :, pl.ds(0, TOP)] = patterns_v[...]

    def meta_z(step):
        at = (z + NZ - step) % NZ
        to = [remote(mz.at[at], mz.at[at], m_send.at[step], m_recv.at[step], dev_z(zr))]
        if step < 3:
            at = (z + step) % NZ
            i = 4 + step
            to.append(remote(mz.at[at], mz.at[at], m_send.at[i], m_recv.at[i], dev_z(zl)))
        for q in to:
            q.start()
        return to

    m_z = [meta_z(0)]
    w[...] = (coeffs[...].astype(jnp.float32) * occ[...]).astype(jnp.bfloat16)

    def compute_tiles(panel, h, s):
        def one(p, carry):
            a = w[left_s[0, s, p]]
            b = panel[right_s[0, s, p]]
            t = lax.dot_general(
                a, b, (((1,), (1,)), ((), ())), preferred_element_type=jnp.float32
            )
            tiles[h, p // 4, p % 4] = t.astype(jnp.bfloat16)
            return carry

        lax.fori_loop(0, NTP, one, 0, unroll=8)

    x1 = {}
    xo = {}
    x2c = {}
    top, low = pl.ds(0, 2), pl.ds(2, 2)

    def x1_start(h):
        x1[h] = (
            remote(tiles.at[h, x2, top], x1_l.at[h], x_send.at[h, 0], x_recv.at[h, 0], dev_x(xr)),
            remote(tiles.at[h, x2, low], x1_r.at[h], x_send.at[h, 1], x_recv.at[h, 1], dev_x(xl)),
        )
        xo[h] = (
            remote(
                tiles.at[h, xr, low], x2_l.at[h, low], x_send.at[h, 4], x_recv.at[h, 4], dev_x(xr)
            ),
            remote(
                tiles.at[h, xl, top], x2_r.at[h, top], x_send.at[h, 5], x_recv.at[h, 5], dev_x(xl)
            ),
        )
        for q in x1[h] + xo[h]:
            q.start()

    def x2_start(h):
        to_r = remote(
            tiles.at[h, xr, top], x2_l.at[h, top], x_send.at[h, 2], x_recv.at[h, 2], dev_x(xr)
        )
        to_l = remote(
            tiles.at[h, xl, low], x2_r.at[h, low], x_send.at[h, 3], x_recv.at[h, 3], dev_x(xl)
        )
        for part, dst, got, first, second in (
            (top, xr, x1_l, x1[h][0], to_r),
            (low, xl, x1_r, x1[h][1], to_l),
        ):
            first.wait_recv()
            tiles[h, dst, part] = (
                tiles[h, dst, part].astype(jnp.float32) + got[h].astype(jnp.float32)
            ).astype(jnp.bfloat16)
            second.start()
        x2c[h] = (to_r, to_l)

    def z_copy(h, i):
        to = 2 * i + h % 2
        return remote(
            zs.at[h, i], rz.at[h // 2, z], z_send.at[h, i], z_recv.at[h // 2, z], dev_z(to)
        )

    def z_start(h):
        for q in xo[h] + x2c[h]:
            q.wait_recv()
        for i in range(4):
            total = (
                tiles[h, x, i].astype(jnp.float32)
                + x2_l[h, i].astype(jnp.float32)
                + x2_r[h, i].astype(jnp.float32)
            ).astype(jnp.bfloat16)
            zs[h, i] = total
            to = 2 * i + h % 2

            @pl.when(z != to)
            def _():
                z_copy(h, i).start()

            @pl.when(z == to)
            def _():
                rz[h // 2, z] = total

    def z_drain(h):
        for i in range(4):

            @pl.when(z != 2 * i + h % 2)
            def _():
                z_copy(h, i).wait_send()

    sj = z % 2
    si = z // 2

    def panel_of(k, j):
        if k == 0:
            a, b = 2 * y + c, 2 * y + oc
        elif k == 1:
            a, b = 2 * ym + c, 2 * yp + oc
        elif k == 2:
            a, b = 2 * yp + c, 2 * ym + oc
        else:
            a, b = 2 * y2 + c, 2 * y2 + oc
        return a if j == 0 else b

    def my_panel(k):
        return panel_of(k, 0) * (1 - sj) + panel_of(k, 1) * sj

    def collocate(k):
        for zf in range(NZ):

            @pl.when(z != zf)
            def _():
                remote(
                    rz.at[k, zf], rz.at[k, zf], z_send.at[0, 0], z_recv.at[k, zf], dev_z(zf)
                ).wait_recv()

        block = jnp.sum(rz[k].astype(jnp.float32), axis=0).astype(jnp.bfloat16)
        s = my_panel(k)
        p = 4 * x + si
        same = jnp.logical_and(s == r, left_s[0, s, p] == right_s[0, s, p])
        scale = jnp.where(same, 1.0, 2.0).astype(jnp.float32)

        def one(t, carry):
            pa = meta_s[k, 1, 2 * si, t]
            pb = meta_s[k, 1, 2 * si + 1, t]
            for ch in range(G // CHUNK):
                cols = pl.ds(ch * CHUNK, CHUNK)
                prod = jnp.dot(block, basis[pb, :, cols], preferred_element_type=jnp.float32)
                row = jnp.sum(basis[pa, :, cols].astype(jnp.float32) * prod, axis=0, keepdims=True)
                row = row * scale
                for q in range(CHUNK // GL):
                    terms[k, t, pl.ds(ch * (CHUNK // GL) + q, 1), :] = row[:, q * GL : (q + 1) * GL]
            return carry

        lax.fori_loop(0, TOP, one, 0, unroll=True)
        vals = [terms[k, t] for t in range(TOP)]
        own = [meta_s[k, 0, si, t] for t in range(TOP)]

        def place(o, carry):
            acc = jnp.zeros((GS, GL), jnp.float32)
            for t in range(TOP):
                acc = jnp.where(own[t] == o, vals[t], acc)
            send_e[k, o] = acc.astype(jnp.bfloat16)
            return carry

        lax.fori_loop(0, NX * NZ, place, 0, unroll=4)
        for d in E_ORDER:
            e_copy(k, d).start()
        arr[k, band] = send_e[k, band]

    z_at = [lax.rem(z + d, NZ) for d in range(NZ)]
    x_at = [lax.rem(x + d, NX) for d in range(NX)]

    def e_copy(k, d):
        zz, xx = z_at[d // NX], x_at[d % NX]
        return remote(
            send_e.at[k, zz * NX + xx],
            arr.at[k, band],
            e_send.at[k],
            e_recv.at[k],
            dev_at(zz, xx),
        )

    def e_all(k):
        others = pl.ds(0, NX * NZ - 1)
        return remote(send_e.at[k, others], arr.at[k, others], e_send.at[k], e_recv.at[k], sib)

    def finish(k, acc):
        e_all(k).wait_recv()

        def one(i, acc):
            zf, xf = i // NX, i % NX
            jj = zf % 2
            ii = zf // 2
            s = panel_of(k, 0) * (1 - jj) + panel_of(k, 1) * jj
            val = arr[k, i].astype(jnp.float32)
            slot = hits[xf * NZ + s, pl.ds(ii, 1), :]
            return tuple(acc[b] + jnp.where(slot == float(b), val, 0.0) for b in range(NBR))

        return lax.fori_loop(0, NX * NZ, one, acc, unroll=4)

    pieces = halves[:1] + (pl.ds(4, 2), pl.ds(6, 2))

    def to_sibling(src, dst, v, at):
        q = remote(src.at[v], dst.at[v], g_send.at[at], g_recv.at[at], sib)
        q.start()
        return q

    compute_tiles(coeffs, 0, panel_of(0, 0))
    x1_start(0)
    g_s.wait_recv()
    compute_tiles(b0, 1, panel_of(0, 1))
    x1_start(1)

    def next_meta(step):
        for q in m_z[step - 1]:
            q.wait_recv()
        if step < 4:
            m_z.append(meta_z(step))

    next_meta(1)
    x2_start(0)
    g_p[0].wait_recv()
    for q in g_m:
        q.start()
    g_fs = [to_sibling(f_a, f_b, halves[0], 5)]
    next_meta(2)
    x2_start(1)
    next_meta(3)

    g_p[1].wait_recv()
    g_fs.append(to_sibling(f_a, f_b, halves[1], 6))
    compute_tiles(f_a, 2, panel_of(1, 0))
    x1_start(2)
    next_meta(4)
    locals_ = []
    for k in range(4):
        q = pltpu.make_async_copy(mz.at[my_panel(k)], meta_s.at[k], l_sem.at[k])
        q.start()
        locals_.append(q)
    mall[x] = mz[:, 0]
    m_x = [
        remote(mall.at[x], mall.at[x], m_send.at[7 + i], m_recv.at[7 + i], dev_x(to))
        for i, to in enumerate((xr, xl))
    ]
    for q in m_x:
        q.start()
    z_start(0)
    for q in g_fs:
        q.wait_recv()
    compute_tiles(f_b, 3, panel_of(1, 1))
    x1_start(3)
    g_m[0].wait_recv()
    g_f = [
        remote(f_a.at[v], t_a.at[v], g_send.at[7 + i], g_recv.at[7 + i], dyp)
        for i, v in enumerate(pieces)
    ]
    for q in g_f:
        q.start()
    g_ms = [to_sibling(s_a, s_b, halves[0], 10)]
    z_start(1)
    x2_start(2)
    x2_start(3)
    for q in m_x:
        q.wait_recv()
    m_x.append(remote(mall.at[xl], mall.at[xl], m_send.at[9], m_recv.at[9], dev_x(xr)))
    m_x[2].start()
    for q in locals_:
        q.wait()
    loads[7].wait()

    g_m[1].wait_recv()
    g_ms.append(to_sibling(s_a, s_b, halves[1], 11))
    compute_tiles(s_a, 4, panel_of(2, 0))
    x1_start(4)
    z_start(2)
    for q in g_ms:
        q.wait_recv()
    compute_tiles(s_b, 5, panel_of(2, 1))
    x1_start(5)
    g_f[0].wait_recv()
    g_ts = [to_sibling(t_a, t_b, pieces[0], 12)]
    z_start(3)
    x2_start(4)
    collocate(0)
    x2_start(5)
    m_x[2].wait_recv()
    lane = lax.broadcasted_iota(jnp.int32, (NX * NZ, 8, 128), 2)
    every = mall[...].reshape(NX * NZ, 8, 128)
    slots = pltpu.roll(every, 4, axis=1)
    mine = jnp.logical_and(lane < TOP, every == band)
    found = jnp.where(mine, slots + 1, 0).astype(jnp.bfloat16).reshape(NX * NZ * 8, 128)
    ones = jnp.ones((128, 128), jnp.bfloat16)
    found = jnp.dot(found, ones, preferred_element_type=jnp.float32) - 1.0
    hits[...] = found.reshape(NX * NZ, 8, 128)

    for i in (1, 2):
        g_f[i].wait_recv()
        g_ts.append(to_sibling(t_a, t_b, pieces[i], 12 + i))
    compute_tiles(t_a, 6, panel_of(3, 0))
    x1_start(6)
    for q in g_ts:
        q.wait_recv()
    compute_tiles(t_b, 7, panel_of(3, 1))
    x1_start(7)
    z_start(4)
    z_start(5)
    x2_start(6)
    x2_start(7)
    collocate(1)
    z_start(6)
    z_start(7)
    collocate(2)
    acc = tuple(jnp.zeros((GS, GL), jnp.float32) for _ in range(NBR))
    acc = finish(0, acc)
    acc = finish(1, acc)
    collocate(3)
    acc = finish(2, acc)
    acc = finish(3, acc)
    for b in range(NBR):
        for q in range(GS):
            out[pl.ds(b, 1), pl.ds(q * GL, GL)] = acc[b][q : q + 1, :]

    pending += [g_s] + g_p + g_m + g_fs + g_f + g_ms + g_ts + m_x + sum(m_z, [])
    for h in range(8):
        pending += list(x1[h] + xo[h] + x2c[h])
    for q in pending:
        q.wait_send()
    for h in range(8):
        z_drain(h)
    for k in range(4):
        e_all(k).wait_send()


def body(coeffs, occupation, tile_left, tile_right, owners, brick_slot, patterns, basis_table):
    hbm = pl.BlockSpec(memory_space=pltpu.HBM)
    bf, f32 = jnp.bfloat16, jnp.float32
    panel = pltpu.VMEM((BLOCKS, BS, KD), bf)
    dma = pltpu.SemaphoreType.DMA
    out = pl.pallas_call(
        kernel,
        out_shape=jax.ShapeDtypeStruct((NBR, G), f32),
        in_specs=[hbm] * 8,
        out_specs=pl.BlockSpec(memory_space=pltpu.VMEM),
        scratch_shapes=[
            panel,
            pltpu.VMEM((1, KD), f32),
            pltpu.VMEM((4, BS, G), bf),
        ]
        + [panel] * 8
        + [
            pltpu.VMEM((8, NX, 4, BS, BS), bf),
            pltpu.VMEM((8, 2, BS, BS), bf),
            pltpu.VMEM((8, 2, BS, BS), bf),
            pltpu.VMEM((8, 4, BS, BS), bf),
            pltpu.VMEM((8, 4, BS, BS), bf),
            pltpu.VMEM((8, 4, BS, BS), bf),
            pltpu.VMEM((4, NZ, BS, BS), bf),
            pltpu.VMEM((4, TOP, GS, GL), f32),
            pltpu.VMEM((4, NX * NZ, GS, GL), bf),
            pltpu.VMEM((4, NX * NZ, GS, GL), bf),
            pltpu.VMEM((4, TOP), jnp.int32),
            pltpu.VMEM((4, TOP), jnp.int32),
            pltpu.VMEM((8, TOP), jnp.int32),
            pltpu.VMEM((NZ, 2, 8, 128), jnp.int32),
            pltpu.VMEM((NX, NZ, 8, 128), jnp.int32),
            pltpu.VMEM((NX * NZ, 8, 128), f32),
            pltpu.SMEM((4, 2, 8, 128), jnp.int32),
            pltpu.SMEM((1, 8, NTP), jnp.int32),
            pltpu.SMEM((1, 8, NTP), jnp.int32),
            dma((15,)),
            dma((15,)),
            dma((8, 6)),
            dma((8, 6)),
            dma((8, 4)),
            dma((4, NZ)),
            dma((4,)),
            dma((4,)),
            dma((10,)),
            dma((10,)),
            dma((4,)),
            dma((8,)),
        ],
        compiler_params=pltpu.CompilerParams(
            collective_id=0, has_side_effects=True, vmem_limit_bytes=VMEM
        ),
        cost_estimate=pl.CostEstimate(
            flops=4 * 10**9, bytes_accessed=4 * 10**6, transcendentals=0
        ),
    )(
        coeffs.reshape(BLOCKS, BS, KD),
        occupation.reshape(1, KD),
        tile_left,
        tile_right,
        owners,
        brick_slot,
        jnp.transpose(patterns, (0, 2, 1)).reshape(8, TOP),
        basis_table,
    )
    return out


def solution(mesh):
    return jax.shard_map(
        body,
        mesh=mesh,
        in_specs=(
            P("row", "band"),
            P("band"),
            P("row", None, None),
            P("row", None, None),
            P(("row", "band"), None),
            P(("row", "band"), None),
            P(("row", "band"), None, None),
            P(),
        ),
        out_specs=P(("row", "band"), None),
        check_vma=False,
    )
```

```python
import jax
import jax.numpy as jnp
from jax import lax
from jax.experimental import pallas as pl
from jax.experimental.pallas import tpu as pltpu
from jax.sharding import PartitionSpec as P

BS = 128
NBR = 8
TOP = 6
G = 2048
GS, GL = 16, 128
NTP = 16
BLOCKS = 8
KD = 512
NX, NY, NZ = 4, 4, 8
CHUNK = 512
Z_ORDER = (4, 3, 5, 2, 6, 1, 7)
X_ORDER = (2, 1, 3)
E_ORDER = tuple(zz * NX + xx for zz in Z_ORDER + (0,) for xx in (2, 1, 3, 0) if zz or xx)
VMEM = 62 * 2**20
MESH = pl.DeviceIdType.MESH


def kernel(
    coeffs_hbm,
    occ_hbm,
    left_hbm,
    right_hbm,
    owners_hbm,
    slots_hbm,
    patterns_hbm,
    basis_hbm,
    out,
    coeffs,
    occ,
    basis,
    w,
    b0,
    f_a,
    f_b,
    s_a,
    s_b,
    t_a,
    t_b,
    tiles,
    x1_l,
    x1_r,
    x2_l,
    x2_r,
    zs,
    rz,
    terms,
    send_e,
    arr,
    owners_v,
    slots_v,
    patterns_v,
    mz,
    mall,
    hits,
    meta_s,
    left_s,
    right_s,
    g_send,
    g_recv,
    x_send,
    x_recv,
    z_send,
    z_recv,
    e_send,
    e_recv,
    m_send,
    m_recv,
    l_sem,
    i_sem,
):
    r = lax.axis_index("row")
    band = lax.axis_index("band")
    y, c = r // 2, r % 2
    z, x = band // NX, band % NX
    sg = 1 - 2 * c
    yp, ym, y2 = (y + sg + NY) % NY, (y - sg + NY) % NY, (y + 2) % NY
    oc = 1 - c
    xr, xl, x2 = (x + 1) % NX, (x + 3) % NX, (x + 2) % NX

    zr, zl = (z + 1) % NZ, (z + NZ - 1) % NZ

    def dev_row(rr):
        return (rr, band)

    def dev_x(xx):
        return (r, z * NX + xx)

    def dev_at(zz, xx):
        return (r, zz * NX + xx)

    def dev_z(zz):
        return (r, zz * NX + x)

    sib = dev_row(2 * y + oc)
    dyp = dev_row(2 * yp + c)
    dym = dev_row(2 * ym + c)

    def remote(src, dst, ss, rs, dev):
        return pltpu.make_async_remote_copy(
            src_ref=src, dst_ref=dst, send_sem=ss, recv_sem=rs, device_id=dev, device_id_type=MESH
        )

    barrier = pltpu.get_barrier_semaphore()
    peers = [sib, dyp, dym]
    peers += [dev_x(xr), dev_x(xl), dev_z(zr), dev_z(zl)]
    for p in peers:
        pl.semaphore_signal(barrier, inc=1, device_id=p, device_id_type=MESH)

    loads = [
        pltpu.make_async_copy(src, dst, i_sem.at[i])
        for i, (src, dst) in enumerate(
            (
                (coeffs_hbm, coeffs),
                (occ_hbm, occ),
                (left_hbm, left_s),
                (right_hbm, right_s),
                (owners_hbm, owners_v),
                (slots_hbm, slots_v),
                (patterns_hbm, patterns_v),
                (basis_hbm, basis),
            )
        )
    ]
    for q in loads:
        q.start()
    pl.semaphore_wait(barrier, len(peers))

    pending = []
    pieces = (pl.ds(0, 4), pl.ds(4, 2), pl.ds(6, 2))
    halves = (pl.ds(0, BLOCKS // 2), pl.ds(BLOCKS // 2, BLOCKS // 2))
    g_s = remote(coeffs_hbm, b0, g_send.at[0], g_recv.at[0], sib)
    g_p = [
        remote(coeffs_hbm.at[v], f_a.at[v], g_send.at[15 + i], g_recv.at[15 + i], dyp)
        for i, v in enumerate(pieces)
    ]
    g_m = [
        remote(coeffs_hbm.at[v], s_a.at[v], g_send.at[18 + i], g_recv.at[18 + i], dym)
        for i, v in enumerate(pieces)
    ]
    for q in g_p + [g_s]:
        q.start()
    for q in loads[:7]:
        q.wait()
    mz[z] = jnp.zeros((2, 8, 128), jnp.int32)
    mz[z, 0, pl.ds(0, 4), pl.ds(0, TOP)] = owners_v[...]
    mz[z, 0, pl.ds(4, 4), pl.ds(0, TOP)] = slots_v[...]
    mz[z, 1, :, pl.ds(0, TOP)] = patterns_v[...]

    def meta_z(step):
        at = (z + NZ - step) % NZ
        to = [remote(mz.at[at], mz.at[at], m_send.at[step], m_recv.at[step], dev_z(zr))]
        if step < 3:
            at = (z + step) % NZ
            i = 4 + step
            to.append(remote(mz.at[at], mz.at[at], m_send.at[i], m_recv.at[i], dev_z(zl)))
        for q in to:
            q.start()
        return to

    m_z = [meta_z(0)]
    w[...] = (coeffs[...].astype(jnp.float32) * occ[...]).astype(jnp.bfloat16)

    def compute_tiles(panel, h, s):
        def one(p, carry):
            a = w[left_s[0, s, p]]
            b = panel[right_s[0, s, p]]
            t = lax.dot_general(
                a, b, (((1,), (1,)), ((), ())), preferred_element_type=jnp.float32
            )
            tiles[h, p // 4, p % 4] = t.astype(jnp.bfloat16)
            return carry

        lax.fori_loop(0, NTP, one, 0, unroll=8)

    x1 = {}
    xo = {}
    x2c = {}
    top, low = pl.ds(0, 2), pl.ds(2, 2)

    def x1_start(h):
        x1[h] = (
            remote(tiles.at[h, x2, top], x1_l.at[h], x_send.at[h, 0], x_recv.at[h, 0], dev_x(xr)),
            remote(tiles.at[h, x2, low], x1_r.at[h], x_send.at[h, 1], x_recv.at[h, 1], dev_x(xl)),
        )
        xo[h] = (
            remote(
                tiles.at[h, xr, low], x2_l.at[h, low], x_send.at[h, 4], x_recv.at[h, 4], dev_x(xr)
            ),
            remote(
                tiles.at[h, xl, top], x2_r.at[h, top], x_send.at[h, 5], x_recv.at[h, 5], dev_x(xl)
            ),
        )
        for q in x1[h] + xo[h]:
            q.start()

    def x2_start(h):
        to_r = remote(
            tiles.at[h, xr, top], x2_l.at[h, top], x_send.at[h, 2], x_recv.at[h, 2], dev_x(xr)
        )
        to_l = remote(
            tiles.at[h, xl, low], x2_r.at[h, low], x_send.at[h, 3], x_recv.at[h, 3], dev_x(xl)
        )
        for part, dst, got, first, second in (
            (top, xr, x1_l, x1[h][0], to_r),
            (low, xl, x1_r, x1[h][1], to_l),
        ):
            first.wait_recv()
            tiles[h, dst, part] = (
                tiles[h, dst, part].astype(jnp.float32) + got[h].astype(jnp.float32)
            ).astype(jnp.bfloat16)
            second.start()
        x2c[h] = (to_r, to_l)

    def z_copy(h, i):
        to = 2 * i + h % 2
        return remote(
            zs.at[h, i], rz.at[h // 2, z], z_send.at[h, i], z_recv.at[h // 2, z], dev_z(to)
        )

    def z_start(h):
        for q in xo[h] + x2c[h]:
            q.wait_recv()
        for i in range(4):
            total = (
                tiles[h, x, i].astype(jnp.float32)
                + x2_l[h, i].astype(jnp.float32)
                + x2_r[h, i].astype(jnp.float32)
            ).astype(jnp.bfloat16)
            zs[h, i] = total
            to = 2 * i + h % 2

            @pl.when(z != to)
            def _():
                z_copy(h, i).start()

            @pl.when(z == to)
            def _():
                rz[h // 2, z] = total

    def z_drain(h):
        for i in range(4):

            @pl.when(z != 2 * i + h % 2)
            def _():
                z_copy(h, i).wait_send()

    sj = z % 2
    si = z // 2

    def panel_of(k, j):
        if k == 0:
            a, b = 2 * y + c, 2 * y + oc
        elif k == 1:
            a, b = 2 * ym + c, 2 * yp + oc
        elif k == 2:
            a, b = 2 * yp + c, 2 * ym + oc
        else:
            a, b = 2 * y2 + c, 2 * y2 + oc
        return a if j == 0 else b

    def my_panel(k):
        return panel_of(k, 0) * (1 - sj) + panel_of(k, 1) * sj

    def collocate(k):
        for zf in range(NZ):

            @pl.when(z != zf)
            def _():
                remote(
                    rz.at[k, zf], rz.at[k, zf], z_send.at[0, 0], z_recv.at[k, zf], dev_z(zf)
                ).wait_recv()

        block = jnp.sum(rz[k].astype(jnp.float32), axis=0).astype(jnp.bfloat16)
        s = my_panel(k)
        p = 4 * x + si
        same = jnp.logical_and(s == r, left_s[0, s, p] == right_s[0, s, p])
        scale = jnp.where(same, 1.0, 2.0).astype(jnp.float32)

        def one(t, carry):
            pa = meta_s[k, 1, 2 * si, t]
            pb = meta_s[k, 1, 2 * si + 1, t]
            for ch in range(G // CHUNK):
                cols = pl.ds(ch * CHUNK, CHUNK)
                prod = jnp.dot(block, basis[pb, :, cols], preferred_element_type=jnp.float32)
                row = jnp.sum(basis[pa, :, cols].astype(jnp.float32) * prod, axis=0, keepdims=True)
                row = row * scale
                for q in range(CHUNK // GL):
                    terms[k, t, pl.ds(ch * (CHUNK // GL) + q, 1), :] = row[:, q * GL : (q + 1) * GL]
            return carry

        lax.fori_loop(0, TOP, one, 0, unroll=True)
        vals = [terms[k, t] for t in range(TOP)]
        own = [meta_s[k, 0, si, t] for t in range(TOP)]

        def place(o):
            acc = jnp.zeros((GS, GL), jnp.float32)
            for t in range(TOP):
                acc = jnp.where(own[t] == o, vals[t], acc)
            send_e[k, o] = acc.astype(jnp.bfloat16)

        for d in E_ORDER:
            place(z_at[d // NX] * NX + x_at[d % NX])
            e_copy(k, d).start()
        place(band)
        arr[k, band] = send_e[k, band]

    z_at = [lax.rem(z + d, NZ) for d in range(NZ)]
    x_at = [lax.rem(x + d, NX) for d in range(NX)]

    def e_copy(k, d):
        zz, xx = z_at[d // NX], x_at[d % NX]
        return remote(
            send_e.at[k, zz * NX + xx],
            arr.at[k, band],
            e_send.at[k],
            e_recv.at[k],
            dev_at(zz, xx),
        )

    def e_all(k):
        others = pl.ds(0, NX * NZ - 1)
        return remote(send_e.at[k, others], arr.at[k, others], e_send.at[k], e_recv.at[k], sib)

    def finish(k, acc):
        e_all(k).wait_recv()

        def one(i, acc):
            zf, xf = i // NX, i % NX
            jj = zf % 2
            ii = zf // 2
            s = panel_of(k, 0) * (1 - jj) + panel_of(k, 1) * jj
            val = arr[k, i].astype(jnp.float32)
            slot = hits[xf * NZ + s, pl.ds(ii, 1), :]
            return tuple(acc[b] + jnp.where(slot == float(b), val, 0.0) for b in range(NBR))

        return lax.fori_loop(0, NX * NZ, one, acc, unroll=4)


    def to_sibling(src, dst, v, at):
        q = remote(src.at[v], dst.at[v], g_send.at[at], g_recv.at[at], sib)
        q.start()
        return q

    compute_tiles(coeffs, 0, panel_of(0, 0))
    x1_start(0)
    g_s.wait_recv()
    compute_tiles(b0, 1, panel_of(0, 1))
    x1_start(1)

    def next_meta(step):
        for q in m_z[step - 1]:
            q.wait_recv()
        if step < 4:
            m_z.append(meta_z(step))

    next_meta(1)
    x2_start(0)
    g_p[0].wait_recv()
    g_fs = [to_sibling(f_a, f_b, halves[0], 5)]
    g_p[1].wait_recv()
    for q in g_m:
        q.start()
    next_meta(2)
    x2_start(1)
    next_meta(3)

    g_p[2].wait_recv()
    g_fs.append(to_sibling(f_a, f_b, halves[1], 6))
    compute_tiles(f_a, 2, panel_of(1, 0))
    x1_start(2)
    next_meta(4)
    locals_ = []
    for k in range(4):
        q = pltpu.make_async_copy(mz.at[my_panel(k)], meta_s.at[k], l_sem.at[k])
        q.start()
        locals_.append(q)
    mall[x] = mz[:, 0]
    m_x = [
        remote(mall.at[x], mall.at[x], m_send.at[7 + i], m_recv.at[7 + i], dev_x(to))
        for i, to in enumerate((xr, xl))
    ]
    for q in m_x:
        q.start()
    z_start(0)
    for q in g_fs:
        q.wait_recv()
    compute_tiles(f_b, 3, panel_of(1, 1))
    x1_start(3)
    g_m[0].wait_recv()
    g_m[1].wait_recv()
    g_f = [
        remote(f_a.at[v], t_a.at[v], g_send.at[7 + i], g_recv.at[7 + i], dyp)
        for i, v in enumerate(pieces)
    ]
    for q in g_f:
        q.start()
    g_ms = [to_sibling(s_a, s_b, halves[0], 10)]
    z_start(1)
    x2_start(2)
    x2_start(3)
    for q in m_x:
        q.wait_recv()
    m_x.append(remote(mall.at[xl], mall.at[xl], m_send.at[9], m_recv.at[9], dev_x(xr)))
    m_x[2].start()
    for q in locals_:
        q.wait()
    loads[7].wait()

    g_m[2].wait_recv()
    g_ms.append(to_sibling(s_a, s_b, halves[1], 11))
    compute_tiles(s_a, 4, panel_of(2, 0))
    x1_start(4)
    z_start(2)
    for q in g_ms:
        q.wait_recv()
    compute_tiles(s_b, 5, panel_of(2, 1))
    x1_start(5)
    g_f[0].wait_recv()
    g_ts = [to_sibling(t_a, t_b, pieces[0], 12)]
    z_start(3)
    x2_start(4)
    collocate(0)
    x2_start(5)
    m_x[2].wait_recv()
    lane = lax.broadcasted_iota(jnp.int32, (NX * NZ, 8, 128), 2)
    every = mall[...].reshape(NX * NZ, 8, 128)
    slots = pltpu.roll(every, 4, axis=1)
    mine = jnp.logical_and(lane < TOP, every == band)
    found = jnp.where(mine, slots + 1, 0).astype(jnp.bfloat16).reshape(NX * NZ * 8, 128)
    ones = jnp.ones((128, 128), jnp.bfloat16)
    found = jnp.dot(found, ones, preferred_element_type=jnp.float32) - 1.0
    hits[...] = found.reshape(NX * NZ, 8, 128)

    for i in (1, 2):
        g_f[i].wait_recv()
        g_ts.append(to_sibling(t_a, t_b, pieces[i], 12 + i))
    compute_tiles(t_a, 6, panel_of(3, 0))
    x1_start(6)
    for q in g_ts:
        q.wait_recv()
    compute_tiles(t_b, 7, panel_of(3, 1))
    x1_start(7)
    z_start(4)
    z_start(5)
    x2_start(6)
    x2_start(7)
    collocate(1)
    z_start(6)
    z_start(7)
    collocate(2)
    acc = tuple(jnp.zeros((GS, GL), jnp.float32) for _ in range(NBR))
    acc = finish(0, acc)
    acc = finish(1, acc)
    collocate(3)
    acc = finish(2, acc)
    acc = finish(3, acc)
    for b in range(NBR):
        for q in range(GS):
            out[pl.ds(b, 1), pl.ds(q * GL, GL)] = acc[b][q : q + 1, :]

    pending += [g_s] + g_p + g_m + g_fs + g_f + g_ms + g_ts + m_x + sum(m_z, [])
    for h in range(8):
        pending += list(x1[h] + xo[h] + x2c[h])
    for q in pending:
        q.wait_send()
    for h in range(8):
        z_drain(h)
    for k in range(4):
        e_all(k).wait_send()


def body(coeffs, occupation, tile_left, tile_right, owners, brick_slot, patterns, basis_table):
    hbm = pl.BlockSpec(memory_space=pltpu.HBM)
    bf, f32 = jnp.bfloat16, jnp.float32
    panel = pltpu.VMEM((BLOCKS, BS, KD), bf)
    dma = pltpu.SemaphoreType.DMA
    out = pl.pallas_call(
        kernel,
        out_shape=jax.ShapeDtypeStruct((NBR, G), f32),
        in_specs=[hbm] * 8,
        out_specs=pl.BlockSpec(memory_space=pltpu.VMEM),
        scratch_shapes=[
            panel,
            pltpu.VMEM((1, KD), f32),
            pltpu.VMEM((4, BS, G), bf),
        ]
        + [panel] * 8
        + [
            pltpu.VMEM((8, NX, 4, BS, BS), bf),
            pltpu.VMEM((8, 2, BS, BS), bf),
            pltpu.VMEM((8, 2, BS, BS), bf),
            pltpu.VMEM((8, 4, BS, BS), bf),
            pltpu.VMEM((8, 4, BS, BS), bf),
            pltpu.VMEM((8, 4, BS, BS), bf),
            pltpu.VMEM((4, NZ, BS, BS), bf),
            pltpu.VMEM((4, TOP, GS, GL), f32),
            pltpu.VMEM((4, NX * NZ, GS, GL), bf),
            pltpu.VMEM((4, NX * NZ, GS, GL), bf),
            pltpu.VMEM((4, TOP), jnp.int32),
            pltpu.VMEM((4, TOP), jnp.int32),
            pltpu.VMEM((8, TOP), jnp.int32),
            pltpu.VMEM((NZ, 2, 8, 128), jnp.int32),
            pltpu.VMEM((NX, NZ, 8, 128), jnp.int32),
            pltpu.VMEM((NX * NZ, 8, 128), f32),
            pltpu.SMEM((4, 2, 8, 128), jnp.int32),
            pltpu.SMEM((1, 8, NTP), jnp.int32),
            pltpu.SMEM((1, 8, NTP), jnp.int32),
            dma((21,)),
            dma((21,)),
            dma((8, 6)),
            dma((8, 6)),
            dma((8, 4)),
            dma((4, NZ)),
            dma((4,)),
            dma((4,)),
            dma((10,)),
            dma((10,)),
            dma((4,)),
            dma((8,)),
        ],
        compiler_params=pltpu.CompilerParams(
            collective_id=0, has_side_effects=True, vmem_limit_bytes=VMEM
        ),
        cost_estimate=pl.CostEstimate(
            flops=4 * 10**9, bytes_accessed=4 * 10**6, transcendentals=0
        ),
    )(
        coeffs.reshape(BLOCKS, BS, KD),
        occupation.reshape(1, KD),
        tile_left,
        tile_right,
        owners,
        brick_slot,
        jnp.transpose(patterns, (0, 2, 1)).reshape(8, TOP),
        basis_table,
    )
    return out


def solution(mesh):
    return jax.shard_map(
        body,
        mesh=mesh,
        in_specs=(
            P("row", "band"),
            P("band"),
            P("row", None, None),
            P("row", None, None),
            P(("row", "band"), None),
            P(("row", "band"), None),
            P(("row", "band"), None, None),
            P(),
        ),
        out_specs=P(("row", "band"), None),
        check_vma=False,
    )
```

```python
import jax
import jax.numpy as jnp
from jax import lax
from jax.experimental import pallas as pl
from jax.experimental.pallas import tpu as pltpu
from jax.sharding import PartitionSpec as P

BS = 128
NBR = 8
TOP = 6
G = 2048
GS, GL = 16, 128
NTP = 16
BLOCKS = 8
KD = 512
NX, NY, NZ = 4, 4, 8
CHUNK = 512
Z_ORDER = (4, 3, 5, 2, 6, 1, 7)
X_ORDER = (2, 1, 3)
E_ORDER = tuple(zz * NX + xx for zz in Z_ORDER + (0,) for xx in (2, 1, 3, 0) if zz or xx)
VMEM = 62 * 2**20
MESH = pl.DeviceIdType.MESH


def kernel(
    coeffs_hbm,
    occ_hbm,
    left_hbm,
    right_hbm,
    owners_hbm,
    slots_hbm,
    patterns_hbm,
    basis_hbm,
    out,
    coeffs,
    occ,
    basis,
    w,
    b0,
    f_a,
    f_b,
    s_a,
    s_b,
    t_a,
    t_b,
    tiles,
    x1_l,
    x1_r,
    x2_l,
    x2_r,
    zs,
    rz,
    terms,
    send_e,
    arr,
    owners_v,
    slots_v,
    patterns_v,
    mz,
    mall,
    hits,
    meta_s,
    left_s,
    right_s,
    g_send,
    g_recv,
    x_send,
    x_recv,
    z_send,
    z_recv,
    e_send,
    e_recv,
    m_send,
    m_recv,
    l_sem,
    i_sem,
):
    r = lax.axis_index("row")
    band = lax.axis_index("band")
    y, c = r // 2, r % 2
    z, x = band // NX, band % NX
    sg = 1 - 2 * c
    yp, ym, y2 = (y + sg + NY) % NY, (y - sg + NY) % NY, (y + 2) % NY
    oc = 1 - c
    xr, xl, x2 = (x + 1) % NX, (x + 3) % NX, (x + 2) % NX

    zr, zl = (z + 1) % NZ, (z + NZ - 1) % NZ

    def dev_row(rr):
        return (rr, band)

    def dev_x(xx):
        return (r, z * NX + xx)

    def dev_at(zz, xx):
        return (r, zz * NX + xx)

    def dev_z(zz):
        return (r, zz * NX + x)

    sib = dev_row(2 * y + oc)
    dyp = dev_row(2 * yp + c)
    dym = dev_row(2 * ym + c)

    def remote(src, dst, ss, rs, dev):
        return pltpu.make_async_remote_copy(
            src_ref=src, dst_ref=dst, send_sem=ss, recv_sem=rs, device_id=dev, device_id_type=MESH
        )

    barrier = pltpu.get_barrier_semaphore()
    peers = [sib, dyp, dym]
    peers += [dev_x(xr), dev_x(xl), dev_z(zr), dev_z(zl)]
    for p in peers:
        pl.semaphore_signal(barrier, inc=1, device_id=p, device_id_type=MESH)

    loads = [
        pltpu.make_async_copy(src, dst, i_sem.at[i])
        for i, (src, dst) in enumerate(
            (
                (coeffs_hbm, coeffs),
                (occ_hbm, occ),
                (left_hbm, left_s),
                (right_hbm, right_s),
                (owners_hbm, owners_v),
                (slots_hbm, slots_v),
                (patterns_hbm, patterns_v),
                (basis_hbm, basis),
            )
        )
    ]
    for q in loads:
        q.start()
    pl.semaphore_wait(barrier, len(peers))

    pending = []
    pieces = (pl.ds(0, 4), pl.ds(4, 2), pl.ds(6, 2))
    halves = (pl.ds(0, BLOCKS // 2), pl.ds(BLOCKS // 2, BLOCKS // 2))
    g_s = remote(coeffs_hbm, b0, g_send.at[0], g_recv.at[0], sib)
    g_p = [
        remote(coeffs_hbm.at[v], f_a.at[v], g_send.at[15 + i], g_recv.at[15 + i], dyp)
        for i, v in enumerate(pieces)
    ]
    g_m = [
        remote(coeffs_hbm.at[v], s_a.at[v], g_send.at[18 + i], g_recv.at[18 + i], dym)
        for i, v in enumerate(pieces)
    ]
    for q in g_p + [g_s]:
        q.start()
    for q in loads[:7]:
        q.wait()
    mz[z] = jnp.zeros((2, 8, 128), jnp.int32)
    mz[z, 0, pl.ds(0, 4), pl.ds(0, TOP)] = owners_v[...]
    mz[z, 0, pl.ds(4, 4), pl.ds(0, TOP)] = slots_v[...]
    mz[z, 1, :, pl.ds(0, TOP)] = patterns_v[...]

    def meta_z(step):
        at = (z + NZ - step) % NZ
        to = [remote(mz.at[at], mz.at[at], m_send.at[step], m_recv.at[step], dev_z(zr))]
        if step < 3:
            at = (z + step) % NZ
            i = 4 + step
            to.append(remote(mz.at[at], mz.at[at], m_send.at[i], m_recv.at[i], dev_z(zl)))
        for q in to:
            q.start()
        return to

    m_z = [meta_z(0)]
    w[...] = (coeffs[...].astype(jnp.float32) * occ[...]).astype(jnp.bfloat16)

    def compute_tiles(panel, h, s):
        def one(p, carry):
            a = w[left_s[0, s, p]]
            b = panel[right_s[0, s, p]]
            t = lax.dot_general(
                a, b, (((1,), (1,)), ((), ())), preferred_element_type=jnp.float32
            )
            tiles[h, p // 4, p % 4] = t.astype(jnp.bfloat16)
            return carry

        lax.fori_loop(0, NTP, one, 0, unroll=8)

    x1 = {}
    xo = {}
    x2c = {}
    top, low = pl.ds(0, 2), pl.ds(2, 2)

    def x1_start(h):
        x1[h] = (
            remote(tiles.at[h, x2, top], x1_l.at[h], x_send.at[h, 0], x_recv.at[h, 0], dev_x(xr)),
            remote(tiles.at[h, x2, low], x1_r.at[h], x_send.at[h, 1], x_recv.at[h, 1], dev_x(xl)),
        )
        xo[h] = (
            remote(
                tiles.at[h, xr, low], x2_l.at[h, low], x_send.at[h, 4], x_recv.at[h, 4], dev_x(xr)
            ),
            remote(
                tiles.at[h, xl, top], x2_r.at[h, top], x_send.at[h, 5], x_recv.at[h, 5], dev_x(xl)
            ),
        )
        for q in x1[h] + xo[h]:
            q.start()

    def x2_start(h):
        to_r = remote(
            tiles.at[h, xr, top], x2_l.at[h, top], x_send.at[h, 2], x_recv.at[h, 2], dev_x(xr)
        )
        to_l = remote(
            tiles.at[h, xl, low], x2_r.at[h, low], x_send.at[h, 3], x_recv.at[h, 3], dev_x(xl)
        )
        for part, dst, got, first, second in (
            (top, xr, x1_l, x1[h][0], to_r),
            (low, xl, x1_r, x1[h][1], to_l),
        ):
            first.wait_recv()
            tiles[h, dst, part] = (
                tiles[h, dst, part].astype(jnp.float32) + got[h].astype(jnp.float32)
            ).astype(jnp.bfloat16)
            second.start()
        x2c[h] = (to_r, to_l)

    def z_copy(h, i):
        to = 2 * i + h % 2
        return remote(
            zs.at[h, i], rz.at[h // 2, z], z_send.at[h, i], z_recv.at[h // 2, z], dev_z(to)
        )

    def z_start(h):
        for q in xo[h] + x2c[h]:
            q.wait_recv()
        for i in range(4):
            total = (
                tiles[h, x, i].astype(jnp.float32)
                + x2_l[h, i].astype(jnp.float32)
                + x2_r[h, i].astype(jnp.float32)
            ).astype(jnp.bfloat16)
            zs[h, i] = total
            to = 2 * i + h % 2

            @pl.when(z != to)
            def _():
                z_copy(h, i).start()

            @pl.when(z == to)
            def _():
                rz[h // 2, z] = total

    def z_drain(h):
        for i in range(4):

            @pl.when(z != 2 * i + h % 2)
            def _():
                z_copy(h, i).wait_send()

    sj = z % 2
    si = z // 2

    def panel_of(k, j):
        if k == 0:
            a, b = 2 * y + c, 2 * y + oc
        elif k == 1:
            a, b = 2 * ym + c, 2 * yp + oc
        elif k == 2:
            a, b = 2 * yp + c, 2 * ym + oc
        else:
            a, b = 2 * y2 + c, 2 * y2 + oc
        return a if j == 0 else b

    def my_panel(k):
        return panel_of(k, 0) * (1 - sj) + panel_of(k, 1) * sj

    def collocate(k):
        for zf in range(NZ):

            @pl.when(z != zf)
            def _():
                remote(
                    rz.at[k, zf], rz.at[k, zf], z_send.at[0, 0], z_recv.at[k, zf], dev_z(zf)
                ).wait_recv()

        block = jnp.sum(rz[k].astype(jnp.float32), axis=0).astype(jnp.bfloat16)
        s = my_panel(k)
        p = 4 * x + si
        same = jnp.logical_and(s == r, left_s[0, s, p] == right_s[0, s, p])
        scale = jnp.where(same, 1.0, 2.0).astype(jnp.float32)

        def one(t, carry):
            pa = meta_s[k, 1, 2 * si, t]
            pb = meta_s[k, 1, 2 * si + 1, t]
            for ch in range(G // CHUNK):
                cols = pl.ds(ch * CHUNK, CHUNK)
                prod = jnp.dot(block, basis[pb, :, cols], preferred_element_type=jnp.float32)
                row = jnp.sum(basis[pa, :, cols].astype(jnp.float32) * prod, axis=0, keepdims=True)
                row = row * scale
                for q in range(CHUNK // GL):
                    terms[k, t, pl.ds(ch * (CHUNK // GL) + q, 1), :] = row[:, q * GL : (q + 1) * GL]
            return carry

        lax.fori_loop(0, TOP, one, 0, unroll=True)
        vals = [terms[k, t] for t in range(TOP)]
        own = [meta_s[k, 0, si, t] for t in range(TOP)]

        def place(o):
            acc = jnp.zeros((GS, GL), jnp.float32)
            for t in range(TOP):
                acc = jnp.where(own[t] == o, vals[t], acc)
            send_e[k, o] = acc.astype(jnp.bfloat16)

        for d in E_ORDER:
            place(z_at[d // NX] * NX + x_at[d % NX])
            e_copy(k, d).start()
        place(band)
        arr[k, band] = send_e[k, band]

    z_at = [lax.rem(z + d, NZ) for d in range(NZ)]
    x_at = [lax.rem(x + d, NX) for d in range(NX)]

    def e_copy(k, d):
        zz, xx = z_at[d // NX], x_at[d % NX]
        return remote(
            send_e.at[k, zz * NX + xx],
            arr.at[k, band],
            e_send.at[k],
            e_recv.at[k],
            dev_at(zz, xx),
        )

    def e_all(k):
        others = pl.ds(0, NX * NZ - 1)
        return remote(send_e.at[k, others], arr.at[k, others], e_send.at[k], e_recv.at[k], sib)

    def finish(k, acc):
        e_all(k).wait_recv()

        def one(i, acc):
            zf, xf = i // NX, i % NX
            jj = zf % 2
            ii = zf // 2
            s = panel_of(k, 0) * (1 - jj) + panel_of(k, 1) * jj
            val = arr[k, i].astype(jnp.float32)
            slot = hits[xf * NZ + s, pl.ds(ii, 1), :]
            return tuple(acc[b] + jnp.where(slot == float(b), val, 0.0) for b in range(NBR))

        return lax.fori_loop(0, NX * NZ, one, acc, unroll=4)


    def to_sibling(src, dst, v, at):
        q = remote(src.at[v], dst.at[v], g_send.at[at], g_recv.at[at], sib)
        q.start()
        return q

    compute_tiles(coeffs, 0, panel_of(0, 0))
    x1_start(0)
    g_s.wait_recv()
    compute_tiles(b0, 1, panel_of(0, 1))
    x1_start(1)

    def next_meta(step):
        for q in m_z[step - 1]:
            q.wait_recv()
        if step < 4:
            m_z.append(meta_z(step))

    next_meta(1)
    x2_start(0)
    g_p[0].wait_recv()
    g_fs = [to_sibling(f_a, f_b, halves[0], 5)]
    g_p[1].wait_recv()
    for q in g_m:
        q.start()
    next_meta(2)
    x2_start(1)
    next_meta(3)

    g_p[2].wait_recv()
    g_fs.append(to_sibling(f_a, f_b, halves[1], 6))
    compute_tiles(f_a, 2, panel_of(1, 0))
    x1_start(2)
    next_meta(4)
    locals_ = []
    for k in range(4):
        q = pltpu.make_async_copy(mz.at[my_panel(k)], meta_s.at[k], l_sem.at[k])
        q.start()
        locals_.append(q)
    mall[x] = mz[:, 0]
    m_x = [
        remote(mall.at[x], mall.at[x], m_send.at[7 + i], m_recv.at[7 + i], dev_x(to))
        for i, to in enumerate((xr, xl))
    ]
    for q in m_x:
        q.start()
    z_start(0)
    for q in g_fs:
        q.wait_recv()
    compute_tiles(f_b, 3, panel_of(1, 1))
    x1_start(3)
    g_m[0].wait_recv()
    g_m[1].wait_recv()
    g_f = [
        remote(f_a.at[v], t_a.at[v], g_send.at[7 + i], g_recv.at[7 + i], dyp)
        for i, v in enumerate(pieces)
    ]
    for q in g_f:
        q.start()
    g_ms = [to_sibling(s_a, s_b, halves[0], 10)]
    z_start(1)
    x2_start(2)
    x2_start(3)
    for q in m_x:
        q.wait_recv()
    m_x.append(remote(mall.at[xl], mall.at[xl], m_send.at[9], m_recv.at[9], dev_x(xr)))
    m_x[2].start()
    for q in locals_:
        q.wait()
    loads[7].wait()

    g_m[2].wait_recv()
    g_ms.append(to_sibling(s_a, s_b, halves[1], 11))
    compute_tiles(s_a, 4, panel_of(2, 0))
    x1_start(4)
    z_start(2)
    for q in g_ms:
        q.wait_recv()
    compute_tiles(s_b, 5, panel_of(2, 1))
    x1_start(5)
    g_f[0].wait_recv()
    g_ts = [to_sibling(t_a, t_b, pieces[0], 12)]
    z_start(3)
    x2_start(4)
    collocate(0)
    x2_start(5)
    m_x[2].wait_recv()
    lane = lax.broadcasted_iota(jnp.int32, (NX * NZ, 8, 128), 2)
    every = mall[...].reshape(NX * NZ, 8, 128)
    slots = pltpu.roll(every, 4, axis=1)
    mine = jnp.logical_and(lane < TOP, every == band)
    found = jnp.where(mine, slots + 1, 0).astype(jnp.bfloat16).reshape(NX * NZ * 8, 128)
    ones = jnp.ones((128, 128), jnp.bfloat16)
    found = jnp.dot(found, ones, preferred_element_type=jnp.float32) - 1.0
    hits[...] = found.reshape(NX * NZ, 8, 128)

    for i in (1, 2):
        g_f[i].wait_recv()
        g_ts.append(to_sibling(t_a, t_b, pieces[i], 12 + i))
    compute_tiles(t_a, 6, panel_of(3, 0))
    x1_start(6)
    for q in g_ts:
        q.wait_recv()
    compute_tiles(t_b, 7, panel_of(3, 1))
    x1_start(7)
    z_start(4)
    z_start(5)
    x2_start(6)
    x2_start(7)
    collocate(1)
    z_start(6)
    z_start(7)
    collocate(2)
    acc = tuple(jnp.zeros((GS, GL), jnp.float32) for _ in range(NBR))
    acc = finish(0, acc)
    acc = finish(1, acc)
    pending += [g_s] + g_p + g_m + g_fs + g_f + g_ms + g_ts + m_x + sum(m_z, [])
    for h in range(8):
        pending += list(x1[h] + xo[h] + x2c[h])
    for q in pending:
        q.wait_send()
    for h in range(7):
        z_drain(h)
    for k in (0, 1):
        e_all(k).wait_send()
    collocate(3)
    acc = finish(2, acc)
    acc = finish(3, acc)
    for b in range(NBR):
        for q in range(GS):
            out[pl.ds(b, 1), pl.ds(q * GL, GL)] = acc[b][q : q + 1, :]

    z_drain(7)
    for k in (2, 3):
        e_all(k).wait_send()


def body(coeffs, occupation, tile_left, tile_right, owners, brick_slot, patterns, basis_table):
    hbm = pl.BlockSpec(memory_space=pltpu.HBM)
    bf, f32 = jnp.bfloat16, jnp.float32
    panel = pltpu.VMEM((BLOCKS, BS, KD), bf)
    dma = pltpu.SemaphoreType.DMA
    out = pl.pallas_call(
        kernel,
        out_shape=jax.ShapeDtypeStruct((NBR, G), f32),
        in_specs=[hbm] * 8,
        out_specs=pl.BlockSpec(memory_space=pltpu.VMEM),
        scratch_shapes=[
            panel,
            pltpu.VMEM((1, KD), f32),
            pltpu.VMEM((4, BS, G), bf),
        ]
        + [panel] * 8
        + [
            pltpu.VMEM((8, NX, 4, BS, BS), bf),
            pltpu.VMEM((8, 2, BS, BS), bf),
            pltpu.VMEM((8, 2, BS, BS), bf),
            pltpu.VMEM((8, 4, BS, BS), bf),
            pltpu.VMEM((8, 4, BS, BS), bf),
            pltpu.VMEM((8, 4, BS, BS), bf),
            pltpu.VMEM((4, NZ, BS, BS), bf),
            pltpu.VMEM((4, TOP, GS, GL), f32),
            pltpu.VMEM((4, NX * NZ, GS, GL), bf),
            pltpu.VMEM((4, NX * NZ, GS, GL), bf),
            pltpu.VMEM((4, TOP), jnp.int32),
            pltpu.VMEM((4, TOP), jnp.int32),
            pltpu.VMEM((8, TOP), jnp.int32),
            pltpu.VMEM((NZ, 2, 8, 128), jnp.int32),
            pltpu.VMEM((NX, NZ, 8, 128), jnp.int32),
            pltpu.VMEM((NX * NZ, 8, 128), f32),
            pltpu.SMEM((4, 2, 8, 128), jnp.int32),
            pltpu.SMEM((1, 8, NTP), jnp.int32),
            pltpu.SMEM((1, 8, NTP), jnp.int32),
            dma((21,)),
            dma((21,)),
            dma((8, 6)),
            dma((8, 6)),
            dma((8, 4)),
            dma((4, NZ)),
            dma((4,)),
            dma((4,)),
            dma((10,)),
            dma((10,)),
            dma((4,)),
            dma((8,)),
        ],
        compiler_params=pltpu.CompilerParams(
            collective_id=0, has_side_effects=True, vmem_limit_bytes=VMEM
        ),
        cost_estimate=pl.CostEstimate(
            flops=4 * 10**9, bytes_accessed=4 * 10**6, transcendentals=0
        ),
    )(
        coeffs.reshape(BLOCKS, BS, KD),
        occupation.reshape(1, KD),
        tile_left,
        tile_right,
        owners,
        brick_slot,
        jnp.transpose(patterns, (0, 2, 1)).reshape(8, TOP),
        basis_table,
    )
    return out


def solution(mesh):
    return jax.shard_map(
        body,
        mesh=mesh,
        in_specs=(
            P("row", "band"),
            P("band"),
            P("row", None, None),
            P("row", None, None),
            P(("row", "band"), None),
            P(("row", "band"), None),
            P(("row", "band"), None, None),
            P(),
        ),
        out_specs=P(("row", "band"), None),
        check_vma=False,
    )
```
